32 devices in a mesh: groups: 2 (over y), ctx: 4 (over z), dp: 2 (over x), mp: 2 (over core).
Axes of the slice: x: 2, y: 2, z: 4, core: 2. Of those that a mesh axis runs over, the one named last changes fastest.
Arguments:
- byte_ids: int32 [4, 1024], P(('groups', 'dp'), 'ctx'), parts along dimension 0, may hold values from 0 to 255
- lengths: int32 [4], P(('groups', 'dp')), parts along dimension 0, may hold values from 128 to 1024, as said below
- hidden: bfloat16 [4, 256, 768], P(('groups', 'dp'), 'ctx'), parts along dimension 0
- w_qkv: bfloat16 [768, 3, 768], P(None, None, 'mp'), may hold values from -0.21875 to 0.21875
- w_out: bfloat16 [768, 768], P('mp'), may hold values from -0.21875 to 0.21875
- w_up: bfloat16 [4, 768, 768], P(None, None, 'mp'), may hold values from -0.109375 to 0.109375
- w_head: bfloat16 [768, 256], P('mp'), may hold values from -0.21875 to 0.21875
Outputs:
- grad_hidden: bfloat16 [4, 256, 768], P(('groups', 'dp'), 'ctx'), parts along dimension 0
The draws below stay inside these ranges and needn't reach their ends.
There are 2 independent parts, one for each index of `groups`. The reference program is written for one: setup_inputs(seed, part) draws one part's arguments, and reference() takes and returns one part's arrays. A program takes and returns all parts, laid end to end along the dimension named above; an argument that names none is the same for every part. Nothing has to cross between parts.
Inputs may be any that keep to these rules, and one draw needn't show every extreme that they name: `lengths`: each document's valid byte count; in every draw some document is full, with 1024 valid bytes.
All inputs are finite; a program needn't handle non-finite values.
Results may differ from the reference program's by a relative error of at most 0.025.
Values may be sent and summed in bfloat16 or wider, within the bound.
A program may use at most 64 MiB of HBM per device.

```python
import jax
import jax.numpy as jnp
from jax import lax

HEAD_DIM = 64
D = 768
VOCAB = 256
DOCS = 2
POS = 256
BYTES = 1024


def draw_lengths(key, part):
    base_key = jax.random.fold_in(key, part)
    key_one = jax.random.fold_in(base_key, 11)
    key_two = jax.random.fold_in(base_key, 12)
    random_lengths = jax.random.randint(key_one, (DOCS,), BYTES // 8, BYTES + 1, dtype=jnp.int32)
    full_index = jax.random.randint(key_two, (), 0, DOCS, dtype=jnp.int32)
    return jnp.where(jnp.arange(DOCS, dtype=jnp.int32) == full_index, BYTES, random_lengths).astype(jnp.int32)


def draw_hidden(key, part):
    base_key = jax.random.fold_in(key, part)
    key_one = jax.random.fold_in(base_key, 21)
    values = jax.random.normal(key_one, (DOCS, POS, D), jnp.float32)
    return values.astype(jnp.bfloat16)


def place_ends(entries, stream_key, least, top_value):
    index_at = [jax.random.randint(jax.random.fold_in(stream_key, axis), (), 0, length) for axis, length in enumerate(entries.shape)]
    main_axis = entries.shape.index(max(entries.shape))
    neighbour = index_at[:main_axis] + [(index_at[main_axis] + 1) % entries.shape[main_axis]] + index_at[main_axis + 1:]
    return entries.at[tuple(index_at)].set(least).at[tuple(neighbour)].set(top_value)


def levels(stream_key, dims, split, smallest, high):
    def one(dim, parts):
        steps = jax.random.uniform(jax.random.fold_in(jax.random.fold_in(stream_key, 6), dim), (parts,), jnp.float32, smallest / len(split), high / len(split))
        return jnp.repeat(jnp.exp(steps), dims[dim] // parts).reshape((-1,) + (1,) * (len(dims) - dim - 1))

    loudness = one(*split[0])
    for cut in split[1:]:
        loudness = loudness * one(*cut)
    return loudness


def bell_draw(rng, dims, scale, most, split=(), kind=jnp.bfloat16):
    drawn = jax.random.normal(rng, dims, jnp.float32) * scale
    if len(split) > 0:
        drawn = levels(rng, dims, split, -0.22, 0.18) * drawn
    return jnp.clip(drawn, min=-most, max=most).astype(kind)


def setup_inputs(seed: int = 0, part: int = 0) -> dict:
    keys = jax.random.split(jax.random.key(seed), 8)
    part_keys = jax.random.split(jax.random.fold_in(keys[7], part), 8)
    byte_ids = place_ends(jax.random.randint(part_keys[0], (DOCS, BYTES), 0, 256), jax.random.fold_in(part_keys[0], 1), 0, 255).astype(jnp.int32)
    lengths = draw_lengths(jax.random.fold_in(jax.random.fold_in(keys[7], part), 71), part)
    hidden = draw_hidden(jax.random.fold_in(jax.random.fold_in(keys[7], part), 71), part)
    w_qkv = bell_draw(keys[3], (D, 3, D), D ** -0.5, 0.21875, ((2, 2),))
    w_out = bell_draw(keys[4], (D, D), D ** -0.5, 0.21875, ((0, 2),))
    w_up = bell_draw(keys[5], (4, D, D), (4 * D) ** -0.5, 0.109375, ((2, 2),))
    w_head = bell_draw(keys[6], (D, VOCAB), D ** -0.5, 0.21875, ((0, 2),))
    return {"byte_ids": byte_ids, "lengths": lengths, "hidden": hidden, "w_qkv": w_qkv, "w_out": w_out, "w_up": w_up, "w_head": w_head}


def gelu_grad(pre_act, incoming):
    result, pullback = jax.vjp(jax.nn.gelu, pre_act)
    return pullback(incoming)[0]

def document_grad(byte_row, length, inputs, w_qkv, w_out, w_up, w_head):
    rows = inputs.shape[0]
    model_width = inputs.shape[1]
    head_count = model_width // HEAD_DIM
    scaling = HEAD_DIM ** (-0.5)
    byte_rows = 4 * rows
    projected = jnp.dot(inputs, w_qkv.reshape(model_width, 3 * model_width), preferred_element_type=jnp.float32).astype(jnp.bfloat16)
    projected = projected.reshape(rows, 3, head_count, HEAD_DIM)
    queries = projected[:, 0].transpose(1, 0, 2)
    key_rows = projected[:, 1].transpose(1, 0, 2)
    value_rows = projected[:, 2].transpose(1, 0, 2)
    usable = 4 * jnp.arange(rows, dtype=jnp.int32) < length

    def forward_head(triple):
        query_head, key_head, value_head = triple
        scores = jnp.dot(query_head, key_head.T, preferred_element_type=jnp.float32) * scaling
        largest = lax.optimization_barrier(jnp.max(jnp.where(usable[None, :], scores, -1e+30), axis=-1))
        weights = jnp.where(usable[None, :], jnp.exp(scores - largest[:, None]), 0.0)
        totals = lax.optimization_barrier(jnp.sum(weights, axis=-1))
        weighted = jnp.dot(weights.astype(jnp.bfloat16), value_head, preferred_element_type=jnp.float32)
        return (weighted / totals[:, None], largest + jnp.log(totals))
    outputs, log_norm = lax.map(forward_head, (queries, key_rows, value_rows))
    attn = outputs.transpose(1, 0, 2).reshape(rows, model_width).astype(jnp.bfloat16)
    context = (inputs.astype(jnp.float32) + jnp.dot(attn, w_out, preferred_element_type=jnp.float32)).astype(jnp.bfloat16)
    repeated = jnp.repeat(context, 4, axis=0)
    padded = jnp.pad(repeated, ((1, 2), (0, 0)))
    pre_act = jnp.zeros((byte_rows, w_up.shape[2]), jnp.float32)
    for offset in range(4):
        pre_act = pre_act + jnp.dot(padded[offset:offset + byte_rows], w_up[offset], preferred_element_type=jnp.float32)
    activated = jax.nn.gelu(pre_act).astype(jnp.bfloat16)
    logits = jnp.dot(activated, w_head, preferred_element_type=jnp.float32)
    byte_mask = jnp.arange(byte_rows, dtype=jnp.int32) < length
    inverse = 1.0 / length.astype(jnp.float32)
    softmaxed = jax.nn.softmax(logits, axis=-1)
    onehot = (byte_row[:, None] == jnp.arange(VOCAB, dtype=jnp.int32)[None, :]).astype(jnp.float32)
    logit_grad = ((softmaxed - onehot) * jnp.where(byte_mask, inverse, 0.0)[:, None]).astype(jnp.bfloat16)
    act_grad = jnp.dot(logit_grad, w_head.T, preferred_element_type=jnp.float32)
    pre_grad = gelu_grad(pre_act, act_grad).astype(jnp.bfloat16)
    grad_padded = jnp.pad(pre_grad, ((2, 1), (0, 0)))
    context_grad = jnp.zeros((rows, model_width), jnp.float32)
    for offset in range(4):
        window = grad_padded[3 - offset:3 - offset + byte_rows].astype(jnp.float32)
        tap_sum = lax.optimization_barrier(jnp.sum(window.reshape(rows, 4, window.shape[1]), axis=1)).astype(jnp.bfloat16)
        context_grad = context_grad + jnp.dot(tap_sum, w_up[offset].T, preferred_element_type=jnp.float32)
    attn_grad = jnp.dot(context_grad.astype(jnp.bfloat16), w_out.T, preferred_element_type=jnp.float32).astype(jnp.bfloat16)
    attn_grad_heads = attn_grad.reshape(rows, head_count, HEAD_DIM).transpose(1, 0, 2)
    attn_heads = attn.reshape(rows, head_count, HEAD_DIM).transpose(1, 0, 2)
    row_dots = lax.optimization_barrier(jnp.sum(attn_grad_heads.astype(jnp.float32) * attn_heads.astype(jnp.float32), axis=-1))

    def backward_head(items):
        query_head, key_head, value_head, outgrad_head, norm_head, dots_head = items
        scores = jnp.dot(query_head, key_head.T, preferred_element_type=jnp.float32) * scaling
        probs = jnp.where(usable[None, :], jnp.exp(scores - norm_head[:, None]), 0.0)
        product = jnp.dot(outgrad_head, value_head.T, preferred_element_type=jnp.float32)
        score_grad = (probs * (product - dots_head[:, None])).astype(jnp.bfloat16)
        query_grad = (jnp.dot(score_grad, key_head, preferred_element_type=jnp.float32) * scaling).astype(jnp.bfloat16)
        key_grad = (jnp.dot(score_grad.T, query_head, preferred_element_type=jnp.float32) * scaling).astype(jnp.bfloat16)
        value_grad = jnp.dot(probs.astype(jnp.bfloat16).T, outgrad_head, preferred_element_type=jnp.float32).astype(jnp.bfloat16)
        return (query_grad, key_grad, value_grad)
    query_grad, key_grad, value_grad = lax.map(backward_head, (queries, key_rows, value_rows, attn_grad_heads, log_norm, row_dots))
    stacked = jnp.stack([query_grad, key_grad, value_grad], axis=0).transpose(2, 0, 1, 3).reshape(rows, 3 * model_width)
    back_proj = jnp.dot(stacked, w_qkv.reshape(model_width, 3 * model_width).T, preferred_element_type=jnp.float32)
    return (context_grad + back_proj).astype(jnp.bfloat16)

def reference(byte_ids, lengths, hidden, w_qkv, w_out, w_up, w_head):

    def one_document(items):
        byte_row, length, inputs = items
        return document_grad(byte_row, length, inputs, w_qkv, w_out, w_up, w_head)
    return lax.map(one_document, (byte_ids, lengths, hidden))
```

```python
import functools

import jax
import jax.numpy as jnp
from jax import lax
from jax.experimental import pallas as pl
from jax.experimental.pallas import tpu as pltpu
from jax.sharding import PartitionSpec as P

HEAD_DIM = 64


def with_halo(x, sides, width):
    for axis, dim in sides:
        devices, length = (lax.axis_size(axis), x.shape[dim])
        up = [(i, (i + 1) % devices) for i in range(devices - 1)]
        down = [(j, i) for i, j in up]
        last = lax.slice_in_dim(x, length - width, length, axis=dim)
        initial = lax.slice_in_dim(x, 0, width, axis=dim)
        before = lax.ppermute(last, axis, up)
        after = lax.ppermute(initial, axis, down)
        x = jnp.concatenate([before, x, after], axis=dim)
    return x


def pair_sum(values):
    return lax.psum(values, "mp")


def edges(values):
    return with_halo(values, (("ctx", 0),), 1)


def gelu_grad(pre_act, incoming):
    result, pullback = jax.vjp(jax.nn.gelu, pre_act)
    return pullback(incoming)[0]


def general_body(byte_ids, lengths, hidden, w_qkv, w_out, w_up, w_head):
    inputs = hidden[0]
    rows = inputs.shape[0]
    model_width = inputs.shape[1]
    split_width = w_qkv.shape[2]
    own_heads = split_width // HEAD_DIM
    scaling = HEAD_DIM ** (-0.5)
    length = lengths[0]
    my_first = lax.axis_index("ctx") * rows
    byte_rows = 4 * rows
    flat_qkv = w_qkv.reshape(model_width, 3 * split_width)
    projected = jnp.dot(inputs, flat_qkv, preferred_element_type=jnp.float32).astype(jnp.bfloat16)
    projected = projected.reshape(rows, 3, own_heads, HEAD_DIM)
    queries = projected[:, 0]
    key_rows = projected[:, 1]
    value_rows = projected[:, 2]

    def usable(first_row, count):
        return 4 * (first_row + jnp.arange(count, dtype=jnp.int32)) < length

    running = jnp.full((rows, own_heads), -1e30, jnp.float32)
    key_piece = lax.all_gather(key_rows, "ctx", axis=0, tiled=True)
    value_piece = lax.all_gather(value_rows, "ctx", axis=0, tiled=True)
    keep = usable(jnp.int32(0), key_piece.shape[0])[None, None, :]
    scores = (
        jnp.einsum("qhd,khd->qhk", queries, key_piece, preferred_element_type=jnp.float32) * scaling
    )
    newest = jnp.maximum(running, jnp.max(jnp.where(keep, scores, -1e30), axis=-1))
    weights = jnp.where(keep, jnp.exp(scores - newest[..., None]), 0.0)
    totals = jnp.sum(weights, axis=-1)
    weighted = jnp.einsum(
        "qhk,khd->qhd",
        weights.astype(jnp.bfloat16),
        value_piece,
        preferred_element_type=jnp.float32,
    )
    weighted, running, totals = (weighted, newest, totals)
    attn_heads = (weighted / totals[..., None]).astype(jnp.bfloat16)
    attn = attn_heads.reshape(rows, split_width)
    log_norm = running + jnp.log(totals)
    context = (
        inputs.astype(jnp.float32)
        + pair_sum(jnp.dot(attn, w_out, preferred_element_type=jnp.float32))
    ).astype(jnp.bfloat16)
    extended = edges(context)
    tap_outputs = [
        jnp.dot(extended, w_up[tap], preferred_element_type=jnp.float32) for tap in range(4)
    ]
    phases = []
    for phase in range(4):
        phase_sum = jnp.zeros((rows, split_width), jnp.float32)
        for tap in range(4):
            shifted = 1 + (phase + tap - 1) // 4
            phase_sum = phase_sum + tap_outputs[tap][shifted : shifted + rows]
        phases.append(phase_sum)
    pre_act = jnp.stack(phases, axis=1).reshape(byte_rows, split_width)
    activated = jax.nn.gelu(pre_act).astype(jnp.bfloat16)
    logits = pair_sum(jnp.dot(activated, w_head, preferred_element_type=jnp.float32))
    byte_first = lax.axis_index("ctx") * byte_rows
    byte_mask = byte_first + jnp.arange(byte_rows, dtype=jnp.int32) < length
    inverse = 1.0 / length.astype(jnp.float32)
    softmaxed = jax.nn.softmax(logits, axis=-1)
    onehot = (byte_ids[0][:, None] == jnp.arange(logits.shape[1], dtype=jnp.int32)[None, :]).astype(
        jnp.float32
    )
    logit_grad = ((softmaxed - onehot) * jnp.where(byte_mask, inverse, 0.0)[:, None]).astype(
        jnp.bfloat16
    )
    act_grad = jnp.dot(logit_grad, w_head.T, preferred_element_type=jnp.float32)
    pre_grad = gelu_grad(pre_act, act_grad).astype(jnp.bfloat16)
    grad_ext = edges(pre_grad.reshape(rows, 4 * split_width)).reshape(byte_rows + 8, split_width)
    partial_grad = jnp.zeros((rows, model_width), jnp.float32)
    for offset in range(4):
        window = grad_ext[5 - offset : 5 - offset + byte_rows].astype(jnp.float32)
        tap_sum = jnp.sum(window.reshape(rows, 4, split_width), axis=1).astype(jnp.bfloat16)
        partial_grad = partial_grad + jnp.dot(
            tap_sum, w_up[offset].T, preferred_element_type=jnp.float32
        )
    context_grad = pair_sum(partial_grad)
    attn_grad = jnp.dot(
        context_grad.astype(jnp.bfloat16), w_out.T, preferred_element_type=jnp.float32
    ).astype(jnp.bfloat16)
    attn_grad = attn_grad.reshape(rows, own_heads, HEAD_DIM)
    row_dots = jnp.sum(attn_grad.astype(jnp.float32) * attn_heads.astype(jnp.float32), axis=-1)
    key_piece = lax.all_gather(key_rows, "ctx", axis=0, tiled=True)
    value_piece = lax.all_gather(value_rows, "ctx", axis=0, tiled=True)
    keep = usable(jnp.int32(0), key_piece.shape[0])[None, None, :]
    scores = (
        jnp.einsum("qhd,khd->qhk", queries, key_piece, preferred_element_type=jnp.float32) * scaling
    )
    probs = jnp.where(keep, jnp.exp(scores - log_norm[..., None]), 0.0)
    product = jnp.einsum("qhd,khd->qhk", attn_grad, value_piece, preferred_element_type=jnp.float32)
    score_grad = (probs * (product - row_dots[..., None])).astype(jnp.bfloat16)
    query_sum = jnp.einsum(
        "qhk,khd->qhd", score_grad, key_piece, preferred_element_type=jnp.float32
    )
    query_grad = (query_sum * scaling).astype(jnp.bfloat16)
    key_keep = usable(my_first, rows)[None, None, :]
    norm_all, dots_all = (
        lax.all_gather(log_norm, "ctx", axis=0, tiled=True),
        lax.all_gather(row_dots, "ctx", axis=0, tiled=True),
    )
    query_piece = lax.all_gather(queries, "ctx", axis=0, tiled=True)
    outgrad_piece = lax.all_gather(attn_grad, "ctx", axis=0, tiled=True)
    count = query_piece.shape[0]
    scores = (
        jnp.einsum("qhd,khd->qhk", query_piece, key_rows, preferred_element_type=jnp.float32)
        * scaling
    )
    probs = jnp.where(key_keep, jnp.exp(scores - norm_all[..., None]), 0.0)
    product = jnp.einsum(
        "qhd,khd->qhk", outgrad_piece, value_rows, preferred_element_type=jnp.float32
    )
    score_grad = (probs * (product - dots_all[..., None])).astype(jnp.bfloat16)
    key_sum = jnp.einsum(
        "qhk,qhd->khd", score_grad, query_piece, preferred_element_type=jnp.float32
    )
    value_sum = jnp.einsum(
        "qhk,qhd->khd",
        probs.astype(jnp.bfloat16),
        outgrad_piece,
        preferred_element_type=jnp.float32,
    )
    key_sum, value_sum = (key_sum, value_sum)
    key_grad = (key_sum * scaling).astype(jnp.bfloat16)
    value_grad = value_sum.astype(jnp.bfloat16)
    stacked = jnp.stack([query_grad, key_grad, value_grad], axis=1).reshape(rows, 3 * split_width)
    back_proj = pair_sum(jnp.dot(stacked, flat_qkv.T, preferred_element_type=jnp.float32))
    input_grad = (context_grad + back_proj).astype(jnp.bfloat16)
    return input_grad[None]


PAD = 16
HALO = 8
MESH = pl.DeviceIdType.MESH
F32 = jnp.float32
BF16 = jnp.bfloat16


def nn(a, b):
    return jnp.dot(a, b, preferred_element_type=F32)


def nt(a, b):
    return lax.dot_general(a, b, (((1,), (1,)), ((), ())), preferred_element_type=F32)


def tn(a, b):
    return lax.dot_general(a, b, (((0,), (0,)), ((), ())), preferred_element_type=F32)


def kernel(
    n,
    len_ref,
    ids_ref,
    own_ref,
    wqkv_hbm,
    wout_hbm,
    wup_hbm,
    whead_hbm,
    out_ref,
    wqkv,
    wout,
    wup,
    whead,
    hid,
    idc,
    q_all,
    k_all,
    v_all,
    attn_all,
    ln2,
    p_own,
    p_keys,
    dgelu,
    ag_all,
    tx_attn,
    rx_attn,
    tx_log,
    rx_log,
    tx_ctx,
    rx_ctx,
    tx_out,
    rx_out,
    w_sem,
    hs_sem,
    hr_sem,
    fs_sem,
    fr_sem,
    is_sem,
    ir_sem,
    as_sem,
    ar_sem,
    xs_sem,
    xr_sem,
):
    rows, width = own_ref.shape
    half = rows // 2
    total = n * rows
    cols = wout.shape[0]
    pairs = cols // 128
    win = rows + 2 * HALO
    me = lax.axis_index("ctx")
    core = lax.axis_index("mp")
    sibling = {"mp": 1 - core}
    length = len_ref[0]

    loads = [
        pltpu.make_async_copy(src, dst, w_sem.at[i])
        for i, (src, dst) in enumerate(
            ((wqkv_hbm, wqkv), (wout_hbm, wout), (wup_hbm, wup), (whead_hbm, whead))
        )
    ]
    for load in loads:
        load.start()

    barrier = pltpu.get_barrier_semaphore()
    for d in range(1, n):
        pl.semaphore_signal(
            barrier, inc=1, device_id={"ctx": lax.rem(me + d, n)}, device_id_type=MESH
        )
    pl.semaphore_signal(barrier, inc=1, device_id=sibling, device_id_type=MESH)
    pl.semaphore_wait(barrier, n)

    def base(chunk):
        return pl.multiple_of(PAD + chunk * rows, 16)

    def source(d):
        return lax.rem(me + n - d, n)

    def peer(d):
        return {"ctx": lax.rem(me + d, n)}

    my_half = pl.multiple_of(core * half, 16)
    sends = []
    for d in range(1, n):
        copy = pltpu.make_async_remote_copy(
            src_ref=own_ref.at[pl.ds(my_half, half)],
            dst_ref=hid.at[pl.ds(pl.multiple_of(base(me) + my_half, 16), half)],
            send_sem=hs_sem.at[d],
            recv_sem=hr_sem.at[d],
            device_id=peer(d),
            device_id_type=MESH,
        )
        copy.start()
        sends.append(copy)
    position = lax.broadcasted_iota(jnp.int32, (rows, 4 * rows), 0)
    byte = lax.broadcasted_iota(jnp.int32, (rows, 4 * rows), 1)
    values = ids_ref[...].astype(F32)
    lane = lax.broadcasted_iota(jnp.int32, (rows, 128), 1)
    id_columns = jnp.zeros((rows, 128), F32)
    for phase in range(4):
        picked = jnp.where(byte == 4 * position + phase, values, 0.0)
        column = jnp.sum(picked, axis=1, keepdims=True)
        id_columns = jnp.where(lane == phase, column, id_columns)
    idc[0:PAD] = jnp.zeros((PAD, 128), BF16)
    idc[PAD + total : 2 * PAD + total] = jnp.zeros((PAD, 128), BF16)
    idc[pl.ds(base(me), rows)] = id_columns.astype(BF16)
    id_sends = []
    for d in range(1, n):
        block = idc.at[pl.ds(base(me), rows)]
        copy = pltpu.make_async_remote_copy(
            src_ref=block,
            dst_ref=block,
            send_sem=is_sem.at[d],
            recv_sem=ir_sem.at[d],
            device_id=peer(d),
            device_id_type=MESH,
        )
        copy.start()
        id_sends.append(copy)

    for edge in (0, PAD + total):
        hid[edge : edge + PAD] = jnp.zeros((PAD, width), BF16)
        q_all[edge : edge + PAD] = jnp.zeros((PAD, cols), BF16)
    hid[pl.ds(base(me), rows)] = own_ref[...]

    def project(chunk):
        x = hid[pl.ds(base(chunk), rows)]
        at = pl.ds(pl.multiple_of(chunk * rows, 16), rows)
        q_all[pl.ds(base(chunk), rows)] = (nn(x, wqkv[0]).astype(BF16).astype(F32) * 0.125).astype(
            BF16
        )
        k_all[at] = nn(x, wqkv[1]).astype(BF16)
        v_all[at] = nn(x, wqkv[2]).astype(BF16)

    loads[0].wait()
    project(me)
    forwards = []
    for d in range(1, n):
        sends[d - 1].wait_recv()
        block = hid.at[pl.ds(pl.multiple_of(base(source(d)) + my_half, 16), half)]
        copy = pltpu.make_async_remote_copy(
            src_ref=block,
            dst_ref=block,
            send_sem=fs_sem.at[d],
            recv_sem=fr_sem.at[d],
            device_id=sibling,
            device_id_type=MESH,
        )
        copy.start()
        forwards.append(copy)
    for d in range(1, n):
        forwards[d - 1].wait_recv()
        project(source(d))

    low = lax.broadcasted_iota(jnp.int32, (1, 128), 1) < 64
    low16 = jnp.where(low, 1.0, 0.0).astype(BF16)
    high16 = jnp.where(low, 0.0, 1.0).astype(BF16)
    usable = 4 * lax.broadcasted_iota(jnp.int32, (1, total), 1) < length

    def softmax_rows(q, k):
        scores = jnp.where(usable, nt(q, k), -1e30)
        largest = jnp.max(scores, axis=1, keepdims=True)
        weights = jnp.exp(scores - largest)
        totals = jnp.sum(weights, axis=1, keepdims=True)
        return weights, largest, totals

    window = pl.ds(pl.multiple_of(me * rows, 16), rows + 2 * PAD)

    def trimmed(x):
        return x.astype(F32)[PAD - HALO : PAD - HALO + win]

    q_win = trimmed(q_all[window]).astype(BF16)
    parts = []
    for pair in range(pairs):
        at = slice(128 * pair, 128 * pair + 128)
        q, k, v = q_win[:, at], k_all[:, at], v_all[:, at]
        outs = []
        for j, mask in enumerate((low16, high16)):
            weights, largest, totals = softmax_rows(q * mask, k)
            inverse = 1.0 / totals
            outs.append(nn(weights.astype(BF16), v) * inverse)
            p_own[2 * pair + j] = (weights * inverse)[HALO : HALO + rows]
        parts.append(jnp.where(low, outs[0], outs[1]).astype(BF16))
    loads[1].wait()
    tx_attn[...] = nn(jnp.concatenate(parts, axis=1), wout[...])

    def swap(i, tx, rx):
        copy = pltpu.make_async_remote_copy(
            src_ref=tx,
            dst_ref=rx,
            send_sem=xs_sem.at[i],
            recv_sem=xr_sem.at[i],
            device_id=sibling,
            device_id_type=MESH,
        )
        copy.start()
        return copy

    swap_attn = swap(0, tx_attn, rx_attn)
    for pair in range(pairs):
        at = slice(128 * pair, 128 * pair + 128)
        q, k, v = q_all[PAD : PAD + total, at], k_all[:, at], v_all[:, at]
        outs, norms = [], []
        for mask in (low16, high16):
            weights, largest, totals = softmax_rows(q * mask, k)
            outs.append(nn(weights.astype(BF16), v) * (1.0 / totals))
            norms.append(largest + jnp.log(totals))
        attn_all[:, at] = jnp.where(low, outs[0], outs[1]).astype(BF16)
        ln2[pair] = jnp.where(low, norms[0], norms[1])
    loads[2].wait()
    loads[3].wait()
    swap_attn.wait_recv()
    first = me * rows - HALO
    place = first + lax.broadcasted_iota(jnp.int32, (win, 1), 0)
    inside = jnp.logical_and(place >= 0, place < total)
    context = trimmed(hid[window]) + (tx_attn[...] + rx_attn[...])
    context = jnp.where(inside, context, 0.0).astype(BF16)
    y0, y1, y2, y3 = [nn(context, wup[tap]) for tap in range(4)]

    def earlier(x):
        return pltpu.roll(x, 1, 0)

    def later(x):
        return pltpu.roll(x, win - 1, 0)

    y01, y23 = y0 + y1, y2 + y3
    pre = (earlier(y0) + y1 + y23, y01 + y23, y01 + y2 + later(y3), y01 + later(y23))
    c0, c1 = 0.7978845608028654, 0.044715
    for phase in range(4):
        x = pre[phase]
        square = x * x
        th = jnp.tanh(c0 * (x + c1 * (x * square)))
        gate = 0.5 * (1.0 + th)
        active = (x * gate).astype(BF16)
        at = slice(phase * win, phase * win + win)
        tx_log[at] = nn(active, whead[...])
        dgelu[at] = gate + 0.5 * x * (1.0 - th * th) * (c0 * (1.0 + 3.0 * c1 * square))
    swap_log = swap(1, tx_log, rx_log)
    own_keys = pl.ds(pl.multiple_of(me * rows, 16), rows)
    key_place = me * rows + lax.broadcasted_iota(jnp.int32, (1, 128), 1) % rows
    key_usable = 4 * key_place < length
    for pair in range(pairs):
        at = slice(128 * pair, 128 * pair + 128)
        k = k_all[own_keys, at]
        both = jnp.concatenate([k * low16, k * high16], axis=0)
        scores = nt(q_all[PAD : PAD + total, at], both)
        p_keys[pair] = jnp.where(key_usable, jnp.exp(scores - ln2[pair]), 0.0)
    for copy in id_sends:
        copy.wait_recv()
    ids_win = trimmed(idc[window])
    inv_length = 1.0 / jnp.full((1, 1), length, jnp.int32).astype(F32)
    vocab = lax.broadcasted_iota(jnp.int32, (win, whead.shape[1]), 1).astype(F32)
    swap_log.wait_recv()
    grads = []
    for phase in range(4):
        at = slice(phase * win, phase * win + win)
        logits = tx_log[at] + rx_log[at]
        weights = jnp.exp(logits - jnp.max(logits, axis=1, keepdims=True))
        soft = weights * (1.0 / jnp.sum(weights, axis=1, keepdims=True))
        hot = jnp.where(vocab == ids_win[:, phase : phase + 1], 1.0, 0.0)
        counted = jnp.logical_and(inside, 4 * place + phase < length)
        logit_grad = ((soft - hot) * jnp.where(counted, inv_length, 0.0)).astype(BF16)
        grad = nt(logit_grad, whead[...]) * dgelu[at]
        grads.append(grad.astype(BF16).astype(F32))
    g0, g1, g2, g3 = grads
    g01, g23 = g0 + g1, g2 + g3
    taps = (later(g0) + g1 + g23, g01 + g23, earlier(g3) + g01 + g2, earlier(g23) + g01)
    partial = jnp.zeros((rows, width), F32)
    for tap in range(4):
        partial = partial + nt(taps[tap][HALO : HALO + rows].astype(BF16), wup[tap])
    tx_ctx[...] = partial
    swap_ctx = swap(2, tx_ctx, rx_ctx)
    swap_ctx.wait_recv()
    context_grad = tx_ctx[...] + rx_ctx[...]
    ag = nt(context_grad.astype(BF16), wout[...]).astype(BF16)
    ag_all[own_keys] = ag
    ag_sends = []
    for d in range(1, n):
        block = ag_all.at[own_keys]
        copy = pltpu.make_async_remote_copy(
            src_ref=block,
            dst_ref=block,
            send_sem=as_sem.at[d],
            recv_sem=ar_sem.at[d],
            device_id=peer(d),
            device_id_type=MESH,
        )
        copy.start()
        ag_sends.append(copy)

    def head_dots(product):
        first_head = jnp.sum(jnp.where(low, product, 0.0), axis=1, keepdims=True)
        second_head = jnp.sum(jnp.where(low, 0.0, product), axis=1, keepdims=True)
        return first_head, second_head

    q_grads = []
    for pair in range(pairs):
        at = slice(128 * pair, 128 * pair + 128)
        g, k, v = ag[:, at], k_all[:, at], v_all[:, at]
        dots = head_dots(g.astype(F32) * attn_all[own_keys, at].astype(F32))
        outs = []
        for j, mask in enumerate((low16, high16)):
            score_grad = p_own[2 * pair + j] * (nt(g * mask, v) - dots[j])
            outs.append(nn(score_grad.astype(BF16), k))
        q_grads.append((jnp.where(low, outs[0], outs[1]) * 0.125).astype(BF16))
    back = nt(jnp.concatenate(q_grads, axis=1), wqkv[0])
    v_pairs = []
    for pair in range(pairs):
        v = v_all[own_keys, 128 * pair : 128 * pair + 128]
        v_pairs.append(jnp.concatenate([v * low16, v * high16], axis=0))
    k_sums = [jnp.zeros((128, 128), F32) for _ in range(pairs)]
    v_sums = [jnp.zeros((128, 128), F32) for _ in range(pairs)]
    for d in range(n):
        if d > 0:
            ag_sends[d - 1].wait_recv()
        chunk = source(d) if d > 0 else me
        block = pl.ds(pl.multiple_of(chunk * rows, 16), rows)
        for pair in range(pairs):
            at = slice(128 * pair, 128 * pair + 128)
            g = ag_all[block, at]
            dots = head_dots(g.astype(F32) * attn_all[block, at].astype(F32))
            probs = p_keys[pair, block]
            score_grad = probs * (nt(g, v_pairs[pair]) - jnp.where(low, dots[0], dots[1]))
            q = q_all[pl.ds(base(chunk), rows), at]
            k_sums[pair] = k_sums[pair] + tn(score_grad.astype(BF16), q)
            v_sums[pair] = v_sums[pair] + tn(probs.astype(BF16), g)

    def joined(sums):
        return jnp.concatenate(
            [jnp.where(low, s[:rows], s[rows:]).astype(BF16) for s in sums], axis=1
        )

    tx_out[...] = back + nt(joined(k_sums), wqkv[1]) + nt(joined(v_sums), wqkv[2])
    swap_out = swap(3, tx_out, rx_out)
    for copy in sends + forwards + id_sends + ag_sends + [swap_attn, swap_log, swap_ctx]:
        copy.wait_send()
    swap_out.wait()
    out_ref[...] = (context_grad + (tx_out[...] + rx_out[...])).astype(BF16)


def fused_body(byte_ids, lengths, hidden, w_qkv, w_out, w_up, w_head):
    n = lax.axis_size("ctx")
    rows, width = hidden.shape[1:]
    total = n * rows
    cols = w_out.shape[0]
    vocab = w_head.shape[1]
    win = rows + 2 * HALO
    vmem = pl.BlockSpec(memory_space=pltpu.VMEM)
    anywhere = pl.BlockSpec(memory_space=pl.ANY)
    dma = pltpu.SemaphoreType.DMA
    result = pl.pallas_call(
        functools.partial(kernel, n),
        out_shape=jax.ShapeDtypeStruct((rows, width), BF16),
        in_specs=[pl.BlockSpec(memory_space=pltpu.SMEM), vmem, vmem] + [anywhere] * 4,
        out_specs=vmem,
        scratch_shapes=[
            pltpu.VMEM((3, width, cols), BF16),
            pltpu.VMEM((cols, width), BF16),
            pltpu.VMEM((4, width, cols), BF16),
            pltpu.VMEM((cols, vocab), BF16),
            pltpu.VMEM((total + 2 * PAD, width), BF16),
            pltpu.VMEM((total + 2 * PAD, 128), BF16),
            pltpu.VMEM((total + 2 * PAD, cols), BF16),
            pltpu.VMEM((total, cols), BF16),
            pltpu.VMEM((total, cols), BF16),
            pltpu.VMEM((total, cols), BF16),
            pltpu.VMEM((cols // 128, total, 128), F32),
            pltpu.VMEM((cols // 64, rows, total), F32),
            pltpu.VMEM((cols // 128, total, 128), F32),
            pltpu.VMEM((4 * win, cols), F32),
            pltpu.VMEM((total, cols), BF16),
            pltpu.VMEM((win, width), F32),
            pltpu.VMEM((win, width), F32),
            pltpu.VMEM((4 * win, vocab), F32),
            pltpu.VMEM((4 * win, vocab), F32),
            pltpu.VMEM((rows, width), F32),
            pltpu.VMEM((rows, width), F32),
            pltpu.VMEM((rows, width), F32),
            pltpu.VMEM((rows, width), F32),
            dma((4,)),
        ]
        + [dma((n,))] * 8
        + [dma((4,))] * 2,
        compiler_params=pltpu.CompilerParams(
            collective_id=0, has_side_effects=True, vmem_limit_bytes=40 * 1024 * 1024
        ),
    )(
        lengths,
        byte_ids,
        hidden[0],
        jnp.transpose(w_qkv, (1, 0, 2)),
        w_out,
        w_up,
        w_head,
    )
    return result[None]


def fits(mesh, rows, cols):
    return mesh.shape["ctx"] * rows <= 256 and rows == 64 and cols % 128 == 0 and mesh.shape["mp"] == 2


def solution(mesh):
    def body(*arrays):
        rows, cols = arrays[2].shape[1], arrays[4].shape[0]
        chosen = fused_body if fits(mesh, rows, cols) else general_body
        return chosen(*arrays)

    placed = (
        P(("groups", "dp"), "ctx"),
        P(("groups", "dp")),
        P(("groups", "dp"), "ctx", None),
        P(None, None, "mp"),
        P("mp", None),
        P(None, None, "mp"),
        P("mp", None),
    )
    return jax.shard_map(
        body,
        mesh=mesh,
        in_specs=placed,
        out_specs=P(("groups", "dp"), "ctx", None),
        check_vma=False,
    )
```

```python
import functools

import jax
import jax.numpy as jnp
from jax import lax
from jax.experimental import pallas as pl
from jax.experimental.pallas import tpu as pltpu
from jax.sharding import PartitionSpec as P

HEAD_DIM = 64


def with_halo(x, sides, width):
    for axis, dim in sides:
        devices, length = (lax.axis_size(axis), x.shape[dim])
        up = [(i, (i + 1) % devices) for i in range(devices - 1)]
        down = [(j, i) for i, j in up]
        last = lax.slice_in_dim(x, length - width, length, axis=dim)
        initial = lax.slice_in_dim(x, 0, width, axis=dim)
        before = lax.ppermute(last, axis, up)
        after = lax.ppermute(initial, axis, down)
        x = jnp.concatenate([before, x, after], axis=dim)
    return x


def pair_sum(values):
    return lax.psum(values, "mp")


def edges(values):
    return with_halo(values, (("ctx", 0),), 1)


def gelu_grad(pre_act, incoming):
    result, pullback = jax.vjp(jax.nn.gelu, pre_act)
    return pullback(incoming)[0]


def general_body(byte_ids, lengths, hidden, w_qkv, w_out, w_up, w_head):
    inputs = hidden[0]
    rows = inputs.shape[0]
    model_width = inputs.shape[1]
    split_width = w_qkv.shape[2]
    own_heads = split_width // HEAD_DIM
    scaling = HEAD_DIM ** (-0.5)
    length = lengths[0]
    my_first = lax.axis_index("ctx") * rows
    byte_rows = 4 * rows
    flat_qkv = w_qkv.reshape(model_width, 3 * split_width)
    projected = jnp.dot(inputs, flat_qkv, preferred_element_type=jnp.float32).astype(jnp.bfloat16)
    projected = projected.reshape(rows, 3, own_heads, HEAD_DIM)
    queries = projected[:, 0]
    key_rows = projected[:, 1]
    value_rows = projected[:, 2]

    def usable(first_row, count):
        return 4 * (first_row + jnp.arange(count, dtype=jnp.int32)) < length

    running = jnp.full((rows, own_heads), -1e30, jnp.float32)
    key_piece = lax.all_gather(key_rows, "ctx", axis=0, tiled=True)
    value_piece = lax.all_gather(value_rows, "ctx", axis=0, tiled=True)
    keep = usable(jnp.int32(0), key_piece.shape[0])[None, None, :]
    scores = (
        jnp.einsum("qhd,khd->qhk", queries, key_piece, preferred_element_type=jnp.float32) * scaling
    )
    newest = jnp.maximum(running, jnp.max(jnp.where(keep, scores, -1e30), axis=-1))
    weights = jnp.where(keep, jnp.exp(scores - newest[..., None]), 0.0)
    totals = jnp.sum(weights, axis=-1)
    weighted = jnp.einsum(
        "qhk,khd->qhd",
        weights.astype(jnp.bfloat16),
        value_piece,
        preferred_element_type=jnp.float32,
    )
    weighted, running, totals = (weighted, newest, totals)
    attn_heads = (weighted / totals[..., None]).astype(jnp.bfloat16)
    attn = attn_heads.reshape(rows, split_width)
    log_norm = running + jnp.log(totals)
    context = (
        inputs.astype(jnp.float32)
        + pair_sum(jnp.dot(attn, w_out, preferred_element_type=jnp.float32))
    ).astype(jnp.bfloat16)
    extended = edges(context)
    tap_outputs = [
        jnp.dot(extended, w_up[tap], preferred_element_type=jnp.float32) for tap in range(4)
    ]
    phases = []
    for phase in range(4):
        phase_sum = jnp.zeros((rows, split_width), jnp.float32)
        for tap in range(4):
            shifted = 1 + (phase + tap - 1) // 4
            phase_sum = phase_sum + tap_outputs[tap][shifted : shifted + rows]
        phases.append(phase_sum)
    pre_act = jnp.stack(phases, axis=1).reshape(byte_rows, split_width)
    activated = jax.nn.gelu(pre_act).astype(jnp.bfloat16)
    logits = pair_sum(jnp.dot(activated, w_head, preferred_element_type=jnp.float32))
    byte_first = lax.axis_index("ctx") * byte_rows
    byte_mask = byte_first + jnp.arange(byte_rows, dtype=jnp.int32) < length
    inverse = 1.0 / length.astype(jnp.float32)
    softmaxed = jax.nn.softmax(logits, axis=-1)
    onehot = (byte_ids[0][:, None] == jnp.arange(logits.shape[1], dtype=jnp.int32)[None, :]).astype(
        jnp.float32
    )
    logit_grad = ((softmaxed - onehot) * jnp.where(byte_mask, inverse, 0.0)[:, None]).astype(
        jnp.bfloat16
    )
    act_grad = jnp.dot(logit_grad, w_head.T, preferred_element_type=jnp.float32)
    pre_grad = gelu_grad(pre_act, act_grad).astype(jnp.bfloat16)
    grad_ext = edges(pre_grad.reshape(rows, 4 * split_width)).reshape(byte_rows + 8, split_width)
    partial_grad = jnp.zeros((rows, model_width), jnp.float32)
    for offset in range(4):
        window = grad_ext[5 - offset : 5 - offset + byte_rows].astype(jnp.float32)
        tap_sum = jnp.sum(window.reshape(rows, 4, split_width), axis=1).astype(jnp.bfloat16)
        partial_grad = partial_grad + jnp.dot(
            tap_sum, w_up[offset].T, preferred_element_type=jnp.float32
        )
    context_grad = pair_sum(partial_grad)
    attn_grad = jnp.dot(
        context_grad.astype(jnp.bfloat16), w_out.T, preferred_element_type=jnp.float32
    ).astype(jnp.bfloat16)
    attn_grad = attn_grad.reshape(rows, own_heads, HEAD_DIM)
    row_dots = jnp.sum(attn_grad.astype(jnp.float32) * attn_heads.astype(jnp.float32), axis=-1)
    key_piece = lax.all_gather(key_rows, "ctx", axis=0, tiled=True)
    value_piece = lax.all_gather(value_rows, "ctx", axis=0, tiled=True)
    keep = usable(jnp.int32(0), key_piece.shape[0])[None, None, :]
    scores = (
        jnp.einsum("qhd,khd->qhk", queries, key_piece, preferred_element_type=jnp.float32) * scaling
    )
    probs = jnp.where(keep, jnp.exp(scores - log_norm[..., None]), 0.0)
    product = jnp.einsum("qhd,khd->qhk", attn_grad, value_piece, preferred_element_type=jnp.float32)
    score_grad = (probs * (product - row_dots[..., None])).astype(jnp.bfloat16)
    query_sum = jnp.einsum(
        "qhk,khd->qhd", score_grad, key_piece, preferred_element_type=jnp.float32
    )
    query_grad = (query_sum * scaling).astype(jnp.bfloat16)
    key_keep = usable(my_first, rows)[None, None, :]
    norm_all, dots_all = (
        lax.all_gather(log_norm, "ctx", axis=0, tiled=True),
        lax.all_gather(row_dots, "ctx", axis=0, tiled=True),
    )
    query_piece = lax.all_gather(queries, "ctx", axis=0, tiled=True)
    outgrad_piece = lax.all_gather(attn_grad, "ctx", axis=0, tiled=True)
    count = query_piece.shape[0]
    scores = (
        jnp.einsum("qhd,khd->qhk", query_piece, key_rows, preferred_element_type=jnp.float32)
        * scaling
    )
    probs = jnp.where(key_keep, jnp.exp(scores - norm_all[..., None]), 0.0)
    product = jnp.einsum(
        "qhd,khd->qhk", outgrad_piece, value_rows, preferred_element_type=jnp.float32
    )
    score_grad = (probs * (product - dots_all[..., None])).astype(jnp.bfloat16)
    key_sum = jnp.einsum(
        "qhk,qhd->khd", score_grad, query_piece, preferred_element_type=jnp.float32
    )
    value_sum = jnp.einsum(
        "qhk,qhd->khd",
        probs.astype(jnp.bfloat16),
        outgrad_piece,
        preferred_element_type=jnp.float32,
    )
    key_sum, value_sum = (key_sum, value_sum)
    key_grad = (key_sum * scaling).astype(jnp.bfloat16)
    value_grad = value_sum.astype(jnp.bfloat16)
    stacked = jnp.stack([query_grad, key_grad, value_grad], axis=1).reshape(rows, 3 * split_width)
    back_proj = pair_sum(jnp.dot(stacked, flat_qkv.T, preferred_element_type=jnp.float32))
    input_grad = (context_grad + back_proj).astype(jnp.bfloat16)
    return input_grad[None]


PAD = 16
HALO = 8
MESH = pl.DeviceIdType.MESH
F32 = jnp.float32
BF16 = jnp.bfloat16


def nn(a, b):
    return jnp.dot(a, b, preferred_element_type=F32)


def nt(a, b):
    return lax.dot_general(a, b, (((1,), (1,)), ((), ())), preferred_element_type=F32)


def tn(a, b):
    return lax.dot_general(a, b, (((0,), (0,)), ((), ())), preferred_element_type=F32)


def kernel(
    n,
    len_ref,
    ids_hbm,
    own_hbm,
    wqkv_hbm,
    wout_hbm,
    wup_hbm,
    whead_hbm,
    out_ref,
    ids_vmem,
    wqkv,
    wout,
    wup,
    whead,
    hid,
    idc,
    q_all,
    k_all,
    v_all,
    attn_all,
    ln2,
    p_own,
    p_keys,
    dgelu,
    ag_all,
    tx_attn,
    rx_attn,
    tx_log,
    rx_log,
    tx_ctx,
    rx_ctx,
    tx_out,
    rx_out,
    w_sem,
    hs_sem,
    hr_sem,
    fs_sem,
    fr_sem,
    is_sem,
    ir_sem,
    as_sem,
    ar_sem,
    xs_sem,
    xr_sem,
):
    rows, width = own_hbm.shape
    half = rows // 2
    total = n * rows
    cols = wout.shape[0]
    pairs = cols // 128
    win = rows + 2 * HALO
    me = lax.axis_index("ctx")
    core = lax.axis_index("mp")
    sibling = {"mp": 1 - core}
    length = len_ref[0]

    own_rows = pl.ds(pl.multiple_of(PAD + me * rows, 16), rows)
    loads = [
        pltpu.make_async_copy(src, dst, w_sem.at[i])
        for i, (src, dst) in enumerate(
            (
                (ids_hbm, ids_vmem),
                (own_hbm, hid.at[own_rows]),
                (wqkv_hbm, wqkv),
                (wout_hbm, wout),
                (wup_hbm, wup),
                (whead_hbm, whead),
            )
        )
    ]
    for load in loads:
        load.start()

    barrier = pltpu.get_barrier_semaphore()
    for d in range(1, n):
        pl.semaphore_signal(
            barrier, inc=1, device_id={"ctx": lax.rem(me + d, n)}, device_id_type=MESH
        )
    pl.semaphore_signal(barrier, inc=1, device_id=sibling, device_id_type=MESH)
    pl.semaphore_wait(barrier, n)

    def base(chunk):
        return pl.multiple_of(PAD + chunk * rows, 16)

    def source(d):
        return lax.rem(me + n - d, n)

    def peer(d):
        return {"ctx": lax.rem(me + d, n)}

    my_half = pl.multiple_of(core * half, 16)
    sends = []
    for d in range(1, n):
        copy = pltpu.make_async_remote_copy(
            src_ref=own_hbm.at[pl.ds(my_half, half)],
            dst_ref=hid.at[pl.ds(pl.multiple_of(base(me) + my_half, 16), half)],
            send_sem=hs_sem.at[d],
            recv_sem=hr_sem.at[d],
            device_id=peer(d),
            device_id_type=MESH,
        )
        copy.start()
        sends.append(copy)
    position = lax.broadcasted_iota(jnp.int32, (rows, 4 * rows), 0)
    byte = lax.broadcasted_iota(jnp.int32, (rows, 4 * rows), 1)
    loads[0].wait()
    values = ids_vmem[...].astype(F32)
    lane = lax.broadcasted_iota(jnp.int32, (rows, 128), 1)
    id_columns = jnp.zeros((rows, 128), F32)
    for phase in range(4):
        picked = jnp.where(byte == 4 * position + phase, values, 0.0)
        column = jnp.sum(picked, axis=1, keepdims=True)
        id_columns = jnp.where(lane == phase, column, id_columns)
    idc[0:PAD] = jnp.zeros((PAD, 128), BF16)
    idc[PAD + total : 2 * PAD + total] = jnp.zeros((PAD, 128), BF16)
    idc[pl.ds(base(me), rows)] = id_columns.astype(BF16)
    id_sends = []
    for d in range(1, n):
        block = idc.at[pl.ds(base(me), rows)]
        copy = pltpu.make_async_remote_copy(
            src_ref=block,
            dst_ref=block,
            send_sem=is_sem.at[d],
            recv_sem=ir_sem.at[d],
            device_id=peer(d),
            device_id_type=MESH,
        )
        copy.start()
        id_sends.append(copy)

    for edge in (0, PAD + total):
        hid[edge : edge + PAD] = jnp.zeros((PAD, width), BF16)
        q_all[edge : edge + PAD] = jnp.zeros((PAD, cols), BF16)

    def project(chunk):
        x = hid[pl.ds(base(chunk), rows)]
        at = pl.ds(pl.multiple_of(chunk * rows, 16), rows)
        q_all[pl.ds(base(chunk), rows)] = (nn(x, wqkv[0]).astype(BF16).astype(F32) * 0.125).astype(
            BF16
        )
        k_all[at] = nn(x, wqkv[1]).astype(BF16)
        v_all[at] = nn(x, wqkv[2]).astype(BF16)

    loads[1].wait()
    loads[2].wait()
    project(me)
    forwards = []
    for d in range(1, n):
        sends[d - 1].wait_recv()
        block = hid.at[pl.ds(pl.multiple_of(base(source(d)) + my_half, 16), half)]
        copy = pltpu.make_async_remote_copy(
            src_ref=block,
            dst_ref=block,
            send_sem=fs_sem.at[d],
            recv_sem=fr_sem.at[d],
            device_id=sibling,
            device_id_type=MESH,
        )
        copy.start()
        forwards.append(copy)
    for d in range(1, n):
        forwards[d - 1].wait_recv()
        project(source(d))

    low = lax.broadcasted_iota(jnp.int32, (1, 128), 1) < 64
    low16 = jnp.where(low, 1.0, 0.0).astype(BF16)
    high16 = jnp.where(low, 0.0, 1.0).astype(BF16)
    usable = 4 * lax.broadcasted_iota(jnp.int32, (1, total), 1) < length

    def softmax_rows(q, k):
        scores = jnp.where(usable, nt(q, k), -1e30)
        largest = jnp.max(scores, axis=1, keepdims=True)
        weights = jnp.exp(scores - largest)
        totals = jnp.sum(weights, axis=1, keepdims=True)
        return weights, largest, totals

    window = pl.ds(pl.multiple_of(me * rows, 16), rows + 2 * PAD)

    def trimmed(x):
        return x.astype(F32)[PAD - HALO : PAD - HALO + win]

    q_win = trimmed(q_all[window]).astype(BF16)
    parts = []
    for pair in range(pairs):
        at = slice(128 * pair, 128 * pair + 128)
        q, k, v = q_win[:, at], k_all[:, at], v_all[:, at]
        outs = []
        for j, mask in enumerate((low16, high16)):
            weights, largest, totals = softmax_rows(q * mask, k)
            inverse = 1.0 / totals
            outs.append(nn(weights.astype(BF16), v) * inverse)
            p_own[2 * pair + j] = (weights * inverse)[HALO : HALO + rows]
        parts.append(jnp.where(low, outs[0], outs[1]).astype(BF16))
    loads[3].wait()

    swaps = []

    def swap(tx, rx, at):
        copy = pltpu.make_async_remote_copy(
            src_ref=tx.at[at],
            dst_ref=rx.at[at],
            send_sem=xs_sem.at[len(swaps)],
            recv_sem=xr_sem.at[len(swaps)],
            device_id=sibling,
            device_id_type=MESH,
        )
        copy.start()
        swaps.append(copy)
        return copy

    attn_win = jnp.concatenate(parts, axis=1)
    blocks = [slice(at, at + 256) for at in range(0, width, 256)]
    for i, at in enumerate(blocks):
        tx_attn[i] = nn(attn_win, wout[:, at])
        swap(tx_attn, rx_attn, i)
    for pair in range(pairs):
        at = slice(128 * pair, 128 * pair + 128)
        q, k, v = q_all[PAD : PAD + total, at], k_all[:, at], v_all[:, at]
        outs, norms = [], []
        for mask in (low16, high16):
            weights, largest, totals = softmax_rows(q * mask, k)
            outs.append(nn(weights.astype(BF16), v) * (1.0 / totals))
            norms.append(largest + jnp.log(totals))
        attn_all[:, at] = jnp.where(low, outs[0], outs[1]).astype(BF16)
        ln2[pair] = jnp.where(low, norms[0], norms[1])
    loads[4].wait()
    loads[5].wait()
    for copy in swaps:
        copy.wait_recv()
    first = me * rows - HALO
    place = first + lax.broadcasted_iota(jnp.int32, (win, 1), 0)
    inside = jnp.logical_and(place >= 0, place < total)
    added = [tx_attn[i] + rx_attn[i] for i in range(len(blocks))]
    context = trimmed(hid[window]) + jnp.concatenate(added, axis=1)
    context = jnp.where(inside, context, 0.0).astype(BF16)
    y0, y1, y2, y3 = [nn(context, wup[tap]) for tap in range(4)]

    def earlier(x):
        return pltpu.roll(x, 1, 0)

    def later(x):
        return pltpu.roll(x, win - 1, 0)

    y01, y23 = y0 + y1, y2 + y3
    pre = (earlier(y0) + y1 + y23, y01 + y23, y01 + y2 + later(y3), y01 + later(y23))
    c0, c1 = 0.7978845608028654, 0.044715
    log_swaps = []
    for phase in range(4):
        x = pre[phase]
        square = x * x
        th = jnp.tanh(c0 * (x + c1 * (x * square)))
        gate = 0.5 * (1.0 + th)
        active = (x * gate).astype(BF16)
        at = slice(phase * win, phase * win + win)
        tx_log[phase] = nn(active, whead[...])
        log_swaps.append(swap(tx_log, rx_log, phase))
        dgelu[at] = gate + 0.5 * x * (1.0 - th * th) * (c0 * (1.0 + 3.0 * c1 * square))
    own_keys = pl.ds(pl.multiple_of(me * rows, 16), rows)
    key_place = me * rows + lax.broadcasted_iota(jnp.int32, (1, 128), 1) % rows
    key_usable = 4 * key_place < length
    for pair in range(pairs):
        at = slice(128 * pair, 128 * pair + 128)
        k = k_all[own_keys, at]
        both = jnp.concatenate([k * low16, k * high16], axis=0)
        scores = nt(q_all[PAD : PAD + total, at], both)
        p_keys[pair] = jnp.where(key_usable, jnp.exp(scores - ln2[pair]), 0.0)
    for copy in id_sends:
        copy.wait_recv()
    ids_win = trimmed(idc[window])
    inv_length = 1.0 / jnp.full((1, 1), length, jnp.int32).astype(F32)
    vocab = lax.broadcasted_iota(jnp.int32, (win, whead.shape[1]), 1).astype(F32)
    grads = []
    for phase in range(4):
        at = slice(phase * win, phase * win + win)
        log_swaps[phase].wait_recv()
        logits = tx_log[phase] + rx_log[phase]
        weights = jnp.exp(logits - jnp.max(logits, axis=1, keepdims=True))
        soft = weights * (1.0 / jnp.sum(weights, axis=1, keepdims=True))
        hot = jnp.where(vocab == ids_win[:, phase : phase + 1], 1.0, 0.0)
        counted = jnp.logical_and(inside, 4 * place + phase < length)
        logit_grad = ((soft - hot) * jnp.where(counted, inv_length, 0.0)).astype(BF16)
        grad = nt(logit_grad, whead[...]) * dgelu[at]
        grads.append(grad.astype(BF16).astype(F32))
    g0, g1, g2, g3 = grads
    g01, g23 = g0 + g1, g2 + g3
    taps = (later(g0) + g1 + g23, g01 + g23, earlier(g3) + g01 + g2, earlier(g23) + g01)
    taps = [x[HALO : HALO + rows].astype(BF16) for x in taps]
    ctx_swaps = []
    for i, at in enumerate(blocks):
        tx_ctx[i] = (nt(taps[0], wup[0, at]) + nt(taps[1], wup[1, at])) + (
            nt(taps[2], wup[2, at]) + nt(taps[3], wup[3, at])
        )
        ctx_swaps.append(swap(tx_ctx, rx_ctx, i))
    for copy in ctx_swaps:
        copy.wait_recv()
    context_grad = jnp.concatenate([tx_ctx[i] + rx_ctx[i] for i in range(len(blocks))], axis=1)
    ag = nt(context_grad.astype(BF16), wout[...]).astype(BF16)
    ag_all[own_keys] = ag
    ag_sends = []
    for d in range(1, n):
        block = ag_all.at[own_keys]
        copy = pltpu.make_async_remote_copy(
            src_ref=block,
            dst_ref=block,
            send_sem=as_sem.at[d],
            recv_sem=ar_sem.at[d],
            device_id=peer(d),
            device_id_type=MESH,
        )
        copy.start()
        ag_sends.append(copy)

    def head_dots(product):
        first_head = jnp.sum(jnp.where(low, product, 0.0), axis=1, keepdims=True)
        second_head = jnp.sum(jnp.where(low, 0.0, product), axis=1, keepdims=True)
        return first_head, second_head

    q_grads = []
    for pair in range(pairs):
        at = slice(128 * pair, 128 * pair + 128)
        g, k, v = ag[:, at], k_all[:, at], v_all[:, at]
        dots = head_dots(g.astype(F32) * attn_all[own_keys, at].astype(F32))
        outs = []
        for j, mask in enumerate((low16, high16)):
            score_grad = p_own[2 * pair + j] * (nt(g * mask, v) - dots[j])
            outs.append(nn(score_grad.astype(BF16), k))
        q_grads.append((jnp.where(low, outs[0], outs[1]) * 0.125).astype(BF16))
    back = nt(jnp.concatenate(q_grads, axis=1), wqkv[0])
    v_pairs = []
    for pair in range(pairs):
        v = v_all[own_keys, 128 * pair : 128 * pair + 128]
        v_pairs.append(jnp.concatenate([v * low16, v * high16], axis=0))
    k_sums = [jnp.zeros((128, 128), F32) for _ in range(pairs)]
    v_sums = [jnp.zeros((128, 128), F32) for _ in range(pairs)]
    for d in range(n):
        if d > 0:
            ag_sends[d - 1].wait_recv()
        chunk = source(d) if d > 0 else me
        block = pl.ds(pl.multiple_of(chunk * rows, 16), rows)
        for pair in range(pairs):
            at = slice(128 * pair, 128 * pair + 128)
            g = ag_all[block, at]
            dots = head_dots(g.astype(F32) * attn_all[block, at].astype(F32))
            probs = p_keys[pair, block]
            score_grad = probs * (nt(g, v_pairs[pair]) - jnp.where(low, dots[0], dots[1]))
            q = q_all[pl.ds(base(chunk), rows), at]
            k_sums[pair] = k_sums[pair] + tn(score_grad.astype(BF16), q)
            v_sums[pair] = v_sums[pair] + tn(probs.astype(BF16), g)

    def joined(sums):
        return jnp.concatenate(
            [jnp.where(low, s[:rows], s[rows:]).astype(BF16) for s in sums], axis=1
        )

    k_grad, v_grad = joined(k_sums), joined(v_sums)
    out_swaps = []
    for i, at in enumerate(blocks):
        tx_out[i] = back[:, at] + nt(k_grad, wqkv[1, at]) + nt(v_grad, wqkv[2, at])
        out_swaps.append(swap(tx_out, rx_out, i))
    for copy in sends + forwards + id_sends + ag_sends + swaps:
        copy.wait_send()
    for i, at in enumerate(blocks):
        out_swaps[i].wait_recv()
        out_ref[:, at] = (context_grad[:, at] + (tx_out[i] + rx_out[i])).astype(BF16)


def fused_body(byte_ids, lengths, hidden, w_qkv, w_out, w_up, w_head):
    n = lax.axis_size("ctx")
    rows, width = hidden.shape[1:]
    total = n * rows
    cols = w_out.shape[0]
    vocab = w_head.shape[1]
    win = rows + 2 * HALO
    vmem = pl.BlockSpec(memory_space=pltpu.VMEM)
    anywhere = pl.BlockSpec(memory_space=pl.ANY)
    dma = pltpu.SemaphoreType.DMA
    result = pl.pallas_call(
        functools.partial(kernel, n),
        out_shape=jax.ShapeDtypeStruct((rows, width), BF16),
        in_specs=[pl.BlockSpec(memory_space=pltpu.SMEM)] + [anywhere] * 6,
        out_specs=vmem,
        scratch_shapes=[
            pltpu.VMEM((1, 4 * rows), jnp.int32),
            pltpu.VMEM((3, width, cols), BF16),
            pltpu.VMEM((cols, width), BF16),
            pltpu.VMEM((4, width, cols), BF16),
            pltpu.VMEM((cols, vocab), BF16),
            pltpu.VMEM((total + 2 * PAD, width), BF16),
            pltpu.VMEM((total + 2 * PAD, 128), BF16),
            pltpu.VMEM((total + 2 * PAD, cols), BF16),
            pltpu.VMEM((total, cols), BF16),
            pltpu.VMEM((total, cols), BF16),
            pltpu.VMEM((total, cols), BF16),
            pltpu.VMEM((cols // 128, total, 128), F32),
            pltpu.VMEM((cols // 64, rows, total), F32),
            pltpu.VMEM((cols // 128, total, 128), F32),
            pltpu.VMEM((4 * win, cols), F32),
            pltpu.VMEM((total, cols), BF16),
            pltpu.VMEM((width // 256, win, 256), F32),
            pltpu.VMEM((width // 256, win, 256), F32),
            pltpu.VMEM((4, win, vocab), F32),
            pltpu.VMEM((4, win, vocab), F32),
            pltpu.VMEM((width // 256, rows, 256), F32),
            pltpu.VMEM((width // 256, rows, 256), F32),
            pltpu.VMEM((width // 256, rows, 256), F32),
            pltpu.VMEM((width // 256, rows, 256), F32),
            dma((6,)),
        ]
        + [dma((n,))] * 8
        + [dma((3 * (width // 256) + 4,))] * 2,
        compiler_params=pltpu.CompilerParams(
            collective_id=0, has_side_effects=True, vmem_limit_bytes=60 * 1024 * 1024
        ),
    )(
        lengths,
        byte_ids,
        hidden[0],
        jnp.transpose(w_qkv, (1, 0, 2)),
        w_out,
        w_up,
        w_head,
    )
    return result[None]


def fits(mesh, rows, width, cols):
    return mesh.shape["ctx"] * rows <= 256 and rows == 64 and cols % 128 == 0 and width % 256 == 0 and mesh.shape["mp"] == 2


def solution(mesh):
    def body(*arrays):
        (_, rows, width), cols = arrays[2].shape, arrays[4].shape[0]
        chosen = fused_body if fits(mesh, rows, width, cols) else general_body
        return chosen(*arrays)

    placed = (
        P(("groups", "dp"), "ctx"),
        P(("groups", "dp")),
        P(("groups", "dp"), "ctx", None),
        P(None, None, "mp"),
        P("mp", None),
        P(None, None, "mp"),
        P("mp", None),
    )
    return jax.shard_map(
        body,
        mesh=mesh,
        in_specs=placed,
        out_specs=P(("groups", "dp"), "ctx", None),
        check_vma=False,
    )
```

```python
import functools

import jax
import jax.numpy as jnp
from jax import lax
from jax.experimental import pallas as pl
from jax.experimental.pallas import tpu as pltpu
from jax.sharding import PartitionSpec as P

HEAD_DIM = 64


def with_halo(x, sides, width):
    for axis, dim in sides:
        devices, length = (lax.axis_size(axis), x.shape[dim])
        up = [(i, (i + 1) % devices) for i in range(devices - 1)]
        down = [(j, i) for i, j in up]
        last = lax.slice_in_dim(x, length - width, length, axis=dim)
        initial = lax.slice_in_dim(x, 0, width, axis=dim)
        before = lax.ppermute(last, axis, up)
        after = lax.ppermute(initial, axis, down)
        x = jnp.concatenate([before, x, after], axis=dim)
    return x


def pair_sum(values):
    return lax.psum(values, "mp")


def edges(values):
    return with_halo(values, (("ctx", 0),), 1)


def gelu_grad(pre_act, incoming):
    result, pullback = jax.vjp(jax.nn.gelu, pre_act)
    return pullback(incoming)[0]


def general_body(byte_ids, lengths, hidden, w_qkv, w_out, w_up, w_head):
    inputs = hidden[0]
    rows = inputs.shape[0]
    model_width = inputs.shape[1]
    split_width = w_qkv.shape[2]
    own_heads = split_width // HEAD_DIM
    scaling = HEAD_DIM ** (-0.5)
    length = lengths[0]
    my_first = lax.axis_index("ctx") * rows
    byte_rows = 4 * rows
    flat_qkv = w_qkv.reshape(model_width, 3 * split_width)
    projected = jnp.dot(inputs, flat_qkv, preferred_element_type=jnp.float32).astype(jnp.bfloat16)
    projected = projected.reshape(rows, 3, own_heads, HEAD_DIM)
    queries = projected[:, 0]
    key_rows = projected[:, 1]
    value_rows = projected[:, 2]

    def usable(first_row, count):
        return 4 * (first_row + jnp.arange(count, dtype=jnp.int32)) < length

    running = jnp.full((rows, own_heads), -1e30, jnp.float32)
    key_piece = lax.all_gather(key_rows, "ctx", axis=0, tiled=True)
    value_piece = lax.all_gather(value_rows, "ctx", axis=0, tiled=True)
    keep = usable(jnp.int32(0), key_piece.shape[0])[None, None, :]
    scores = (
        jnp.einsum("qhd,khd->qhk", queries, key_piece, preferred_element_type=jnp.float32) * scaling
    )
    newest = jnp.maximum(running, jnp.max(jnp.where(keep, scores, -1e30), axis=-1))
    weights = jnp.where(keep, jnp.exp(scores - newest[..., None]), 0.0)
    totals = jnp.sum(weights, axis=-1)
    weighted = jnp.einsum(
        "qhk,khd->qhd",
        weights.astype(jnp.bfloat16),
        value_piece,
        preferred_element_type=jnp.float32,
    )
    weighted, running, totals = (weighted, newest, totals)
    attn_heads = (weighted / totals[..., None]).astype(jnp.bfloat16)
    attn = attn_heads.reshape(rows, split_width)
    log_norm = running + jnp.log(totals)
    context = (
        inputs.astype(jnp.float32)
        + pair_sum(jnp.dot(attn, w_out, preferred_element_type=jnp.float32))
    ).astype(jnp.bfloat16)
    extended = edges(context)
    tap_outputs = [
        jnp.dot(extended, w_up[tap], preferred_element_type=jnp.float32) for tap in range(4)
    ]
    phases = []
    for phase in range(4):
        phase_sum = jnp.zeros((rows, split_width), jnp.float32)
        for tap in range(4):
            shifted = 1 + (phase + tap - 1) // 4
            phase_sum = phase_sum + tap_outputs[tap][shifted : shifted + rows]
        phases.append(phase_sum)
    pre_act = jnp.stack(phases, axis=1).reshape(byte_rows, split_width)
    activated = jax.nn.gelu(pre_act).astype(jnp.bfloat16)
    logits = pair_sum(jnp.dot(activated, w_head, preferred_element_type=jnp.float32))
    byte_first = lax.axis_index("ctx") * byte_rows
    byte_mask = byte_first + jnp.arange(byte_rows, dtype=jnp.int32) < length
    inverse = 1.0 / length.astype(jnp.float32)
    softmaxed = jax.nn.softmax(logits, axis=-1)
    onehot = (byte_ids[0][:, None] == jnp.arange(logits.shape[1], dtype=jnp.int32)[None, :]).astype(
        jnp.float32
    )
    logit_grad = ((softmaxed - onehot) * jnp.where(byte_mask, inverse, 0.0)[:, None]).astype(
        jnp.bfloat16
    )
    act_grad = jnp.dot(logit_grad, w_head.T, preferred_element_type=jnp.float32)
    pre_grad = gelu_grad(pre_act, act_grad).astype(jnp.bfloat16)
    grad_ext = edges(pre_grad.reshape(rows, 4 * split_width)).reshape(byte_rows + 8, split_width)
    partial_grad = jnp.zeros((rows, model_width), jnp.float32)
    for offset in range(4):
        window = grad_ext[5 - offset : 5 - offset + byte_rows].astype(jnp.float32)
        tap_sum = jnp.sum(window.reshape(rows, 4, split_width), axis=1).astype(jnp.bfloat16)
        partial_grad = partial_grad + jnp.dot(
            tap_sum, w_up[offset].T, preferred_element_type=jnp.float32
        )
    context_grad = pair_sum(partial_grad)
    attn_grad = jnp.dot(
        context_grad.astype(jnp.bfloat16), w_out.T, preferred_element_type=jnp.float32
    ).astype(jnp.bfloat16)
    attn_grad = attn_grad.reshape(rows, own_heads, HEAD_DIM)
    row_dots = jnp.sum(attn_grad.astype(jnp.float32) * attn_heads.astype(jnp.float32), axis=-1)
    key_piece = lax.all_gather(key_rows, "ctx", axis=0, tiled=True)
    value_piece = lax.all_gather(value_rows, "ctx", axis=0, tiled=True)
    keep = usable(jnp.int32(0), key_piece.shape[0])[None, None, :]
    scores = (
        jnp.einsum("qhd,khd->qhk", queries, key_piece, preferred_element_type=jnp.float32) * scaling
    )
    probs = jnp.where(keep, jnp.exp(scores - log_norm[..., None]), 0.0)
    product = jnp.einsum("qhd,khd->qhk", attn_grad, value_piece, preferred_element_type=jnp.float32)
    score_grad = (probs * (product - row_dots[..., None])).astype(jnp.bfloat16)
    query_sum = jnp.einsum(
        "qhk,khd->qhd", score_grad, key_piece, preferred_element_type=jnp.float32
    )
    query_grad = (query_sum * scaling).astype(jnp.bfloat16)
    key_keep = usable(my_first, rows)[None, None, :]
    norm_all, dots_all = (
        lax.all_gather(log_norm, "ctx", axis=0, tiled=True),
        lax.all_gather(row_dots, "ctx", axis=0, tiled=True),
    )
    query_piece = lax.all_gather(queries, "ctx", axis=0, tiled=True)
    outgrad_piece = lax.all_gather(attn_grad, "ctx", axis=0, tiled=True)
    count = query_piece.shape[0]
    scores = (
        jnp.einsum("qhd,khd->qhk", query_piece, key_rows, preferred_element_type=jnp.float32)
        * scaling
    )
    probs = jnp.where(key_keep, jnp.exp(scores - norm_all[..., None]), 0.0)
    product = jnp.einsum(
        "qhd,khd->qhk", outgrad_piece, value_rows, preferred_element_type=jnp.float32
    )
    score_grad = (probs * (product - dots_all[..., None])).astype(jnp.bfloat16)
    key_sum = jnp.einsum(
        "qhk,qhd->khd", score_grad, query_piece, preferred_element_type=jnp.float32
    )
    value_sum = jnp.einsum(
        "qhk,qhd->khd",
        probs.astype(jnp.bfloat16),
        outgrad_piece,
        preferred_element_type=jnp.float32,
    )
    key_sum, value_sum = (key_sum, value_sum)
    key_grad = (key_sum * scaling).astype(jnp.bfloat16)
    value_grad = value_sum.astype(jnp.bfloat16)
    stacked = jnp.stack([query_grad, key_grad, value_grad], axis=1).reshape(rows, 3 * split_width)
    back_proj = pair_sum(jnp.dot(stacked, flat_qkv.T, preferred_element_type=jnp.float32))
    input_grad = (context_grad + back_proj).astype(jnp.bfloat16)
    return input_grad[None]


PAD = 16
HALO = 8
MESH = pl.DeviceIdType.MESH
F32 = jnp.float32
BF16 = jnp.bfloat16


def nn(a, b):
    return jnp.dot(a, b, preferred_element_type=F32)


def nt(a, b):
    return lax.dot_general(a, b, (((1,), (1,)), ((), ())), preferred_element_type=F32)


def tn(a, b):
    return lax.dot_general(a, b, (((0,), (0,)), ((), ())), preferred_element_type=F32)


def kernel(
    n,
    len_ref,
    ids_hbm,
    own_hbm,
    wqkv_hbm,
    wout_hbm,
    wup_hbm,
    whead_hbm,
    out_ref,
    ids,
    wqkv,
    wout,
    wup,
    whead,
    hid,
    q_all,
    k_all,
    v_all,
    attn_all,
    ln2,
    p_own,
    p_keys,
    dgelu,
    ag_all,
    tx_attn,
    rx_attn,
    tx_log,
    rx_log,
    tx_ctx,
    rx_ctx,
    tx_out,
    rx_out,
    w_sem,
    hs_sem,
    hr_sem,
    fs_sem,
    fr_sem,
    is_sem,
    ir_sem,
    as_sem,
    ar_sem,
    xs_sem,
    xr_sem,
):
    rows, width = own_hbm.shape
    half = rows // 2
    total = n * rows
    cols = wout.shape[0]
    pairs = cols // 128
    win = rows + 2 * HALO
    me = lax.axis_index("ctx")
    core = lax.axis_index("mp")
    sibling = {"mp": 1 - core}
    length = len_ref[0]

    own_rows = pl.ds(pl.multiple_of(PAD + me * rows, 16), rows)
    loads = [
        pltpu.make_async_copy(src, dst, w_sem.at[i])
        for i, (src, dst) in enumerate(
            (
                (ids_hbm, ids.at[1]),
                (own_hbm, hid.at[own_rows]),
                (wqkv_hbm, wqkv),
                (wout_hbm, wout),
                (wup_hbm, wup),
                (whead_hbm, whead),
            )
        )
    ]
    for load in loads:
        load.start()

    barrier = pltpu.get_barrier_semaphore()
    for d in range(1, n):
        pl.semaphore_signal(
            barrier, inc=1, device_id={"ctx": lax.rem(me + d, n)}, device_id_type=MESH
        )
    pl.semaphore_signal(barrier, inc=1, device_id=sibling, device_id_type=MESH)
    pl.semaphore_wait(barrier, n)

    def base(chunk):
        return pl.multiple_of(PAD + chunk * rows, 16)

    def source(d):
        return lax.rem(me + n - d, n)

    def peer(d):
        return {"ctx": lax.rem(me + d, n)}

    my_half = pl.multiple_of(core * half, 16)
    sends = []
    for d in range(1, n):
        copy = pltpu.make_async_remote_copy(
            src_ref=own_hbm.at[pl.ds(my_half, half)],
            dst_ref=hid.at[pl.ds(pl.multiple_of(base(me) + my_half, 16), half)],
            send_sem=hs_sem.at[d],
            recv_sem=hr_sem.at[d],
            device_id=peer(d),
            device_id_type=MESH,
        )
        copy.start()
        sends.append(copy)
    id_sends = []
    for d, slot in ((1, 0), (n - 1, 2)):
        copy = pltpu.make_async_remote_copy(
            src_ref=ids_hbm,
            dst_ref=ids.at[slot],
            send_sem=is_sem.at[d],
            recv_sem=ir_sem.at[d],
            device_id=peer(d),
            device_id_type=MESH,
        )
        copy.start()
        id_sends.append(copy)

    for edge in (0, PAD + total):
        hid[edge : edge + PAD] = jnp.zeros((PAD, width), BF16)
        q_all[edge : edge + PAD] = jnp.zeros((PAD, cols), BF16)

    def project(chunk):
        x = hid[pl.ds(base(chunk), rows)]
        at = pl.ds(pl.multiple_of(chunk * rows, 16), rows)
        q_all[pl.ds(base(chunk), rows)] = (nn(x, wqkv[0]).astype(BF16).astype(F32) * 0.125).astype(
            BF16
        )
        k_all[at] = nn(x, wqkv[1]).astype(BF16)
        v_all[at] = nn(x, wqkv[2]).astype(BF16)

    for load in loads[:3]:
        load.wait()
    project(me)
    forwards = []
    for d in range(1, n):
        sends[d - 1].wait_recv()
        block = hid.at[pl.ds(pl.multiple_of(base(source(d)) + my_half, 16), half)]
        copy = pltpu.make_async_remote_copy(
            src_ref=block,
            dst_ref=block,
            send_sem=fs_sem.at[d],
            recv_sem=fr_sem.at[d],
            device_id=sibling,
            device_id_type=MESH,
        )
        copy.start()
        forwards.append(copy)
    for d in range(1, n):
        forwards[d - 1].wait_recv()
        project(source(d))

    low = lax.broadcasted_iota(jnp.int32, (1, 128), 1) < 64
    low16 = jnp.where(low, 1.0, 0.0).astype(BF16)
    high16 = jnp.where(low, 0.0, 1.0).astype(BF16)
    usable = 4 * lax.broadcasted_iota(jnp.int32, (1, total), 1) < length

    def softmax_rows(q, k):
        scores = jnp.where(usable, nt(q, k), -1e30)
        largest = jnp.max(scores, axis=1, keepdims=True)
        weights = jnp.exp(scores - largest)
        totals = jnp.sum(weights, axis=1, keepdims=True)
        return weights, largest, totals

    window = pl.ds(pl.multiple_of(me * rows, 16), rows + 2 * PAD)

    def trimmed(x):
        return x.astype(F32)[PAD - HALO : PAD - HALO + win]

    q_win = trimmed(q_all[window]).astype(BF16)
    parts = []
    for pair in range(pairs):
        at = slice(128 * pair, 128 * pair + 128)
        q, k, v = q_win[:, at], k_all[:, at], v_all[:, at]
        outs = []
        for j, mask in enumerate((low16, high16)):
            weights, largest, totals = softmax_rows(q * mask, k)
            inverse = 1.0 / totals
            outs.append(nn(weights.astype(BF16), v) * inverse)
            p_own[2 * pair + j] = (weights * inverse)[HALO : HALO + rows]
        parts.append(jnp.where(low, outs[0], outs[1]).astype(BF16))
    loads[3].wait()

    swaps = []

    def swap(tx, rx, at):
        copy = pltpu.make_async_remote_copy(
            src_ref=tx.at[at],
            dst_ref=rx.at[at],
            send_sem=xs_sem.at[len(swaps)],
            recv_sem=xr_sem.at[len(swaps)],
            device_id=sibling,
            device_id_type=MESH,
        )
        copy.start()
        swaps.append(copy)
        return copy

    attn_win = jnp.concatenate(parts, axis=1)
    blocks = [slice(at, at + 256) for at in range(0, width, 256)]
    for i, at in enumerate(blocks):
        tx_attn[i] = nn(attn_win, wout[:, at])
        swap(tx_attn, rx_attn, i)
    for pair in range(pairs):
        at = slice(128 * pair, 128 * pair + 128)
        q, k, v = q_all[PAD : PAD + total, at], k_all[:, at], v_all[:, at]
        outs, norms = [], []
        for mask in (low16, high16):
            weights, largest, totals = softmax_rows(q * mask, k)
            outs.append(nn(weights.astype(BF16), v) * (1.0 / totals))
            norms.append(largest + jnp.log(totals))
        attn_all[:, at] = jnp.where(low, outs[0], outs[1]).astype(BF16)
        ln2[pair] = jnp.where(low, norms[0], norms[1])
    loads[4].wait()
    loads[5].wait()
    for copy in swaps:
        copy.wait_recv()
    first = me * rows - HALO
    place = first + lax.broadcasted_iota(jnp.int32, (win, 1), 0)
    inside = jnp.logical_and(place >= 0, place < total)
    added = [tx_attn[i] + rx_attn[i] for i in range(len(blocks))]
    context = trimmed(hid[window]) + jnp.concatenate(added, axis=1)
    context = jnp.where(inside, context, 0.0).astype(BF16)
    y0, y1, y2, y3 = [nn(context, wup[tap]) for tap in range(4)]

    def earlier(x):
        return pltpu.roll(x, 1, 0)

    def later(x):
        return pltpu.roll(x, win - 1, 0)

    y01, y23 = y0 + y1, y2 + y3
    pre = (earlier(y0) + y1 + y23, y01 + y23, y01 + y2 + later(y3), y01 + later(y23))
    c0, c1 = 0.7978845608028654, 0.044715
    log_swaps = []
    for phase in range(4):
        x = pre[phase]
        square = x * x
        th = jnp.tanh(c0 * (x + c1 * (x * square)))
        gate = 0.5 * (1.0 + th)
        active = (x * gate).astype(BF16)
        at = slice(phase * win, phase * win + win)
        tx_log[phase] = nn(active, whead[...])
        log_swaps.append(swap(tx_log, rx_log, phase))
        dgelu[at] = gate + 0.5 * x * (1.0 - th * th) * (c0 * (1.0 + 3.0 * c1 * square))
    own_keys = pl.ds(pl.multiple_of(me * rows, 16), rows)
    key_place = me * rows + lax.broadcasted_iota(jnp.int32, (1, 128), 1) % rows
    key_usable = 4 * key_place < length
    for pair in range(pairs):
        at = slice(128 * pair, 128 * pair + 128)
        k = k_all[own_keys, at]
        both = jnp.concatenate([k * low16, k * high16], axis=0)
        scores = nt(q_all[PAD : PAD + total, at], both)
        p_keys[pair] = jnp.where(key_usable, jnp.exp(scores - ln2[pair]), 0.0)
    for copy in id_sends:
        copy.wait_recv()
    byte = 4 * (lax.broadcasted_iota(jnp.int32, (win, 4 * rows), 0) - HALO)
    offset = byte - lax.broadcasted_iota(jnp.int32, (win, 4 * rows), 1)
    ids_win = []
    for phase in range(4):
        found = jnp.zeros((win, 4 * rows), jnp.int32)
        for side in range(3):
            found = found + jnp.where(offset == 4 * rows * (side - 1) - phase, ids[side], 0)
        ids_win.append(jnp.sum(found.astype(F32), axis=1, keepdims=True))
    inv_length = 1.0 / jnp.full((1, 1), length, jnp.int32).astype(F32)
    vocab = lax.broadcasted_iota(jnp.int32, (win, whead.shape[1]), 1).astype(F32)
    grads = []
    for phase in range(4):
        at = slice(phase * win, phase * win + win)
        log_swaps[phase].wait_recv()
        logits = tx_log[phase] + rx_log[phase]
        weights = jnp.exp(logits - jnp.max(logits, axis=1, keepdims=True))
        soft = weights * (1.0 / jnp.sum(weights, axis=1, keepdims=True))
        hot = jnp.where(vocab == ids_win[phase], 1.0, 0.0)
        counted = jnp.logical_and(inside, 4 * place + phase < length)
        logit_grad = ((soft - hot) * jnp.where(counted, inv_length, 0.0)).astype(BF16)
        grad = nt(logit_grad, whead[...]) * dgelu[at]
        grads.append(grad.astype(BF16).astype(F32))
    g0, g1, g2, g3 = grads
    g01, g23 = g0 + g1, g2 + g3
    taps = (later(g0) + g1 + g23, g01 + g23, earlier(g3) + g01 + g2, earlier(g23) + g01)
    taps = [x[HALO : HALO + rows].astype(BF16) for x in taps]
    ctx_swaps = []
    for i, at in enumerate(blocks):
        tx_ctx[i] = (nt(taps[0], wup[0, at]) + nt(taps[1], wup[1, at])) + (
            nt(taps[2], wup[2, at]) + nt(taps[3], wup[3, at])
        )
        ctx_swaps.append(swap(tx_ctx, rx_ctx, i))
    for copy in ctx_swaps:
        copy.wait_recv()
    context_grad = jnp.concatenate([tx_ctx[i] + rx_ctx[i] for i in range(len(blocks))], axis=1)
    ag = nt(context_grad.astype(BF16), wout[...]).astype(BF16)
    ag_all[own_keys] = ag
    ag_sends = []
    for d in range(1, n):
        block = ag_all.at[own_keys]
        copy = pltpu.make_async_remote_copy(
            src_ref=block,
            dst_ref=block,
            send_sem=as_sem.at[d],
            recv_sem=ar_sem.at[d],
            device_id=peer(d),
            device_id_type=MESH,
        )
        copy.start()
        ag_sends.append(copy)

    def head_dots(product):
        first_head = jnp.sum(jnp.where(low, product, 0.0), axis=1, keepdims=True)
        second_head = jnp.sum(jnp.where(low, 0.0, product), axis=1, keepdims=True)
        return first_head, second_head

    q_grads = []
    for pair in range(pairs):
        at = slice(128 * pair, 128 * pair + 128)
        g, k, v = ag[:, at], k_all[:, at], v_all[:, at]
        dots = head_dots(g.astype(F32) * attn_all[own_keys, at].astype(F32))
        outs = []
        for j, mask in enumerate((low16, high16)):
            score_grad = p_own[2 * pair + j] * (nt(g * mask, v) - dots[j])
            outs.append(nn(score_grad.astype(BF16), k))
        q_grads.append((jnp.where(low, outs[0], outs[1]) * 0.125).astype(BF16))
    back = nt(jnp.concatenate(q_grads, axis=1), wqkv[0])
    v_pairs = []
    for pair in range(pairs):
        v = v_all[own_keys, 128 * pair : 128 * pair + 128]
        v_pairs.append(jnp.concatenate([v * low16, v * high16], axis=0))
    k_sums = [jnp.zeros((128, 128), F32) for _ in range(pairs)]
    v_sums = [jnp.zeros((128, 128), F32) for _ in range(pairs)]
    for d in range(n):
        if d > 0:
            ag_sends[d - 1].wait_recv()
        chunk = source(d) if d > 0 else me
        block = pl.ds(pl.multiple_of(chunk * rows, 16), rows)
        for pair in range(pairs):
            at = slice(128 * pair, 128 * pair + 128)
            g = ag_all[block, at]
            dots = head_dots(g.astype(F32) * attn_all[block, at].astype(F32))
            probs = p_keys[pair, block]
            score_grad = probs * (nt(g, v_pairs[pair]) - jnp.where(low, dots[0], dots[1]))
            q = q_all[pl.ds(base(chunk), rows), at]
            k_sums[pair] = k_sums[pair] + tn(score_grad.astype(BF16), q)
            v_sums[pair] = v_sums[pair] + tn(probs.astype(BF16), g)

    def joined(sums):
        return jnp.concatenate(
            [jnp.where(low, s[:rows], s[rows:]).astype(BF16) for s in sums], axis=1
        )

    k_grad, v_grad = joined(k_sums), joined(v_sums)
    out_swaps = []
    for i, at in enumerate(blocks):
        tx_out[i] = back[:, at] + nt(k_grad, wqkv[1, at]) + nt(v_grad, wqkv[2, at])
        out_swaps.append(swap(tx_out, rx_out, i))
    for copy in sends + forwards + id_sends + ag_sends + swaps:
        copy.wait_send()
    for i, at in enumerate(blocks):
        out_swaps[i].wait_recv()
        out_ref[:, at] = (context_grad[:, at] + (tx_out[i] + rx_out[i])).astype(BF16)


def fused_body(byte_ids, lengths, hidden, w_qkv, w_out, w_up, w_head):
    n = lax.axis_size("ctx")
    rows, width = hidden.shape[1:]
    total = n * rows
    cols = w_out.shape[0]
    vocab = w_head.shape[1]
    win = rows + 2 * HALO
    vmem = pl.BlockSpec(memory_space=pltpu.VMEM)
    anywhere = pl.BlockSpec(memory_space=pl.ANY)
    dma = pltpu.SemaphoreType.DMA
    result = pl.pallas_call(
        functools.partial(kernel, n),
        out_shape=jax.ShapeDtypeStruct((rows, width), BF16),
        in_specs=[pl.BlockSpec(memory_space=pltpu.SMEM)] + [anywhere] * 6,
        out_specs=vmem,
        scratch_shapes=[
            pltpu.VMEM((3, 1, 4 * rows), jnp.int32),
            pltpu.VMEM((3, width, cols), BF16),
            pltpu.VMEM((cols, width), BF16),
            pltpu.VMEM((4, width, cols), BF16),
            pltpu.VMEM((cols, vocab), BF16),
            pltpu.VMEM((total + 2 * PAD, width), BF16),
            pltpu.VMEM((total + 2 * PAD, cols), BF16),
            pltpu.VMEM((total, cols), BF16),
            pltpu.VMEM((total, cols), BF16),
            pltpu.VMEM((total, cols), BF16),
            pltpu.VMEM((cols // 128, total, 128), F32),
            pltpu.VMEM((cols // 64, rows, total), F32),
            pltpu.VMEM((cols // 128, total, 128), F32),
            pltpu.VMEM((4 * win, cols), F32),
            pltpu.VMEM((total, cols), BF16),
            pltpu.VMEM((width // 256, win, 256), F32),
            pltpu.VMEM((width // 256, win, 256), F32),
            pltpu.VMEM((4, win, vocab), F32),
            pltpu.VMEM((4, win, vocab), F32),
            pltpu.VMEM((width // 256, rows, 256), F32),
            pltpu.VMEM((width // 256, rows, 256), F32),
            pltpu.VMEM((width // 256, rows, 256), F32),
            pltpu.VMEM((width // 256, rows, 256), F32),
            dma((6,)),
        ]
        + [dma((n,))] * 8
        + [dma((3 * (width // 256) + 4,))] * 2,
        compiler_params=pltpu.CompilerParams(
            collective_id=0, has_side_effects=True, vmem_limit_bytes=60 * 1024 * 1024
        ),
    )(
        lengths,
        byte_ids,
        hidden[0],
        jnp.transpose(w_qkv, (1, 0, 2)),
        w_out,
        w_up,
        w_head,
    )
    return result[None]


def fits(mesh, rows, width, cols):
    return 3 <= mesh.shape["ctx"] <= 4 and rows == 64 and cols % 128 == 0 and width % 256 == 0 and mesh.shape["mp"] == 2


def solution(mesh):
    def body(*arrays):
        (_, rows, width), cols = arrays[2].shape, arrays[4].shape[0]
        chosen = fused_body if fits(mesh, rows, width, cols) else general_body
        return chosen(*arrays)

    placed = (
        P(("groups", "dp"), "ctx"),
        P(("groups", "dp")),
        P(("groups", "dp"), "ctx", None),
        P(None, None, "mp"),
        P("mp", None),
        P(None, None, "mp"),
        P("mp", None),
    )
    return jax.shard_map(
        body,
        mesh=mesh,
        in_specs=placed,
        out_specs=P(("groups", "dp"), "ctx", None),
        check_vma=False,
    )
```

```python
import functools

import jax
import jax.numpy as jnp
from jax import lax
from jax.experimental import pallas as pl
from jax.experimental.pallas import tpu as pltpu
from jax.sharding import PartitionSpec as P

HEAD_DIM = 64


def with_halo(x, sides, width):
    for axis, dim in sides:
        devices, length = (lax.axis_size(axis), x.shape[dim])
        up = [(i, (i + 1) % devices) for i in range(devices - 1)]
        down = [(j, i) for i, j in up]
        last = lax.slice_in_dim(x, length - width, length, axis=dim)
        initial = lax.slice_in_dim(x, 0, width, axis=dim)
        before = lax.ppermute(last, axis, up)
        after = lax.ppermute(initial, axis, down)
        x = jnp.concatenate([before, x, after], axis=dim)
    return x


def pair_sum(values):
    return lax.psum(values, "mp")


def edges(values):
    return with_halo(values, (("ctx", 0),), 1)


def gelu_grad(pre_act, incoming):
    result, pullback = jax.vjp(jax.nn.gelu, pre_act)
    return pullback(incoming)[0]


def general_body(byte_ids, lengths, hidden, w_qkv, w_out, w_up, w_head):
    inputs = hidden[0]
    rows = inputs.shape[0]
    model_width = inputs.shape[1]
    split_width = w_qkv.shape[2]
    own_heads = split_width // HEAD_DIM
    scaling = HEAD_DIM ** (-0.5)
    length = lengths[0]
    my_first = lax.axis_index("ctx") * rows
    byte_rows = 4 * rows
    flat_qkv = w_qkv.reshape(model_width, 3 * split_width)
    projected = jnp.dot(inputs, flat_qkv, preferred_element_type=jnp.float32).astype(jnp.bfloat16)
    projected = projected.reshape(rows, 3, own_heads, HEAD_DIM)
    queries = projected[:, 0]
    key_rows = projected[:, 1]
    value_rows = projected[:, 2]

    def usable(first_row, count):
        return 4 * (first_row + jnp.arange(count, dtype=jnp.int32)) < length

    running = jnp.full((rows, own_heads), -1e30, jnp.float32)
    key_piece = lax.all_gather(key_rows, "ctx", axis=0, tiled=True)
    value_piece = lax.all_gather(value_rows, "ctx", axis=0, tiled=True)
    keep = usable(jnp.int32(0), key_piece.shape[0])[None, None, :]
    scores = (
        jnp.einsum("qhd,khd->qhk", queries, key_piece, preferred_element_type=jnp.float32) * scaling
    )
    newest = jnp.maximum(running, jnp.max(jnp.where(keep, scores, -1e30), axis=-1))
    weights = jnp.where(keep, jnp.exp(scores - newest[..., None]), 0.0)
    totals = jnp.sum(weights, axis=-1)
    weighted = jnp.einsum(
        "qhk,khd->qhd",
        weights.astype(jnp.bfloat16),
        value_piece,
        preferred_element_type=jnp.float32,
    )
    weighted, running, totals = (weighted, newest, totals)
    attn_heads = (weighted / totals[..., None]).astype(jnp.bfloat16)
    attn = attn_heads.reshape(rows, split_width)
    log_norm = running + jnp.log(totals)
    context = (
        inputs.astype(jnp.float32)
        + pair_sum(jnp.dot(attn, w_out, preferred_element_type=jnp.float32))
    ).astype(jnp.bfloat16)
    extended = edges(context)
    tap_outputs = [
        jnp.dot(extended, w_up[tap], preferred_element_type=jnp.float32) for tap in range(4)
    ]
    phases = []
    for phase in range(4):
        phase_sum = jnp.zeros((rows, split_width), jnp.float32)
        for tap in range(4):
            shifted = 1 + (phase + tap - 1) // 4
            phase_sum = phase_sum + tap_outputs[tap][shifted : shifted + rows]
        phases.append(phase_sum)
    pre_act = jnp.stack(phases, axis=1).reshape(byte_rows, split_width)
    activated = jax.nn.gelu(pre_act).astype(jnp.bfloat16)
    logits = pair_sum(jnp.dot(activated, w_head, preferred_element_type=jnp.float32))
    byte_first = lax.axis_index("ctx") * byte_rows
    byte_mask = byte_first + jnp.arange(byte_rows, dtype=jnp.int32) < length
    inverse = 1.0 / length.astype(jnp.float32)
    softmaxed = jax.nn.softmax(logits, axis=-1)
    onehot = (byte_ids[0][:, None] == jnp.arange(logits.shape[1], dtype=jnp.int32)[None, :]).astype(
        jnp.float32
    )
    logit_grad = ((softmaxed - onehot) * jnp.where(byte_mask, inverse, 0.0)[:, None]).astype(
        jnp.bfloat16
    )
    act_grad = jnp.dot(logit_grad, w_head.T, preferred_element_type=jnp.float32)
    pre_grad = gelu_grad(pre_act, act_grad).astype(jnp.bfloat16)
    grad_ext = edges(pre_grad.reshape(rows, 4 * split_width)).reshape(byte_rows + 8, split_width)
    partial_grad = jnp.zeros((rows, model_width), jnp.float32)
    for offset in range(4):
        window = grad_ext[5 - offset : 5 - offset + byte_rows].astype(jnp.float32)
        tap_sum = jnp.sum(window.reshape(rows, 4, split_width), axis=1).astype(jnp.bfloat16)
        partial_grad = partial_grad + jnp.dot(
            tap_sum, w_up[offset].T, preferred_element_type=jnp.float32
        )
    context_grad = pair_sum(partial_grad)
    attn_grad = jnp.dot(
        context_grad.astype(jnp.bfloat16), w_out.T, preferred_element_type=jnp.float32
    ).astype(jnp.bfloat16)
    attn_grad = attn_grad.reshape(rows, own_heads, HEAD_DIM)
    row_dots = jnp.sum(attn_grad.astype(jnp.float32) * attn_heads.astype(jnp.float32), axis=-1)
    key_piece = lax.all_gather(key_rows, "ctx", axis=0, tiled=True)
    value_piece = lax.all_gather(value_rows, "ctx", axis=0, tiled=True)
    keep = usable(jnp.int32(0), key_piece.shape[0])[None, None, :]
    scores = (
        jnp.einsum("qhd,khd->qhk", queries, key_piece, preferred_element_type=jnp.float32) * scaling
    )
    probs = jnp.where(keep, jnp.exp(scores - log_norm[..., None]), 0.0)
    product = jnp.einsum("qhd,khd->qhk", attn_grad, value_piece, preferred_element_type=jnp.float32)
    score_grad = (probs * (product - row_dots[..., None])).astype(jnp.bfloat16)
    query_sum = jnp.einsum(
        "qhk,khd->qhd", score_grad, key_piece, preferred_element_type=jnp.float32
    )
    query_grad = (query_sum * scaling).astype(jnp.bfloat16)
    key_keep = usable(my_first, rows)[None, None, :]
    norm_all, dots_all = (
        lax.all_gather(log_norm, "ctx", axis=0, tiled=True),
        lax.all_gather(row_dots, "ctx", axis=0, tiled=True),
    )
    query_piece = lax.all_gather(queries, "ctx", axis=0, tiled=True)
    outgrad_piece = lax.all_gather(attn_grad, "ctx", axis=0, tiled=True)
    count = query_piece.shape[0]
    scores = (
        jnp.einsum("qhd,khd->qhk", query_piece, key_rows, preferred_element_type=jnp.float32)
        * scaling
    )
    probs = jnp.where(key_keep, jnp.exp(scores - norm_all[..., None]), 0.0)
    product = jnp.einsum(
        "qhd,khd->qhk", outgrad_piece, value_rows, preferred_element_type=jnp.float32
    )
    score_grad = (probs * (product - dots_all[..., None])).astype(jnp.bfloat16)
    key_sum = jnp.einsum(
        "qhk,qhd->khd", score_grad, query_piece, preferred_element_type=jnp.float32
    )
    value_sum = jnp.einsum(
        "qhk,qhd->khd",
        probs.astype(jnp.bfloat16),
        outgrad_piece,
        preferred_element_type=jnp.float32,
    )
    key_sum, value_sum = (key_sum, value_sum)
    key_grad = (key_sum * scaling).astype(jnp.bfloat16)
    value_grad = value_sum.astype(jnp.bfloat16)
    stacked = jnp.stack([query_grad, key_grad, value_grad], axis=1).reshape(rows, 3 * split_width)
    back_proj = pair_sum(jnp.dot(stacked, flat_qkv.T, preferred_element_type=jnp.float32))
    input_grad = (context_grad + back_proj).astype(jnp.bfloat16)
    return input_grad[None]


PAD = 16
HALO = 8
MESH = pl.DeviceIdType.MESH
F32 = jnp.float32
BF16 = jnp.bfloat16


def nn(a, b):
    return jnp.dot(a, b, preferred_element_type=F32)


def nt(a, b):
    return lax.dot_general(a, b, (((1,), (1,)), ((), ())), preferred_element_type=F32)


def tn(a, b):
    return lax.dot_general(a, b, (((0,), (0,)), ((), ())), preferred_element_type=F32)


def kernel(
    n,
    len_ref,
    ids_hbm,
    own_hbm,
    wqkv_hbm,
    wout_hbm,
    wup_hbm,
    whead_hbm,
    out_ref,
    ids,
    wqkv,
    wout,
    wup,
    whead,
    hid,
    q_all,
    k_all,
    v_all,
    attn_all,
    ln2,
    p_own,
    p_keys,
    dgelu,
    ag_all,
    tx_attn,
    rx_attn,
    tx_log,
    rx_log,
    tx_ctx,
    rx_ctx,
    tx_out,
    rx_out,
    w_sem,
    hs_sem,
    hr_sem,
    fs_sem,
    fr_sem,
    is_sem,
    ir_sem,
    as_sem,
    ar_sem,
    xs_sem,
    xr_sem,
):
    rows, width = own_hbm.shape
    half = rows // 2
    total = n * rows
    cols = wout.shape[0]
    pairs = cols // 128
    win = rows + 2 * HALO
    me = lax.axis_index("ctx")
    core = lax.axis_index("mp")
    sibling = {"mp": 1 - core}
    length = len_ref[0]

    own_rows = pl.ds(pl.multiple_of(PAD + me * rows, 16), rows)
    loads = [
        pltpu.make_async_copy(src, dst, w_sem.at[i])
        for i, (src, dst) in enumerate(
            (
                (ids_hbm, ids.at[1]),
                (own_hbm, hid.at[own_rows]),
                (wqkv_hbm, wqkv),
                (wout_hbm, wout),
                (wup_hbm, wup),
                (whead_hbm, whead),
            )
        )
    ]
    for load in loads:
        load.start()

    barrier = pltpu.get_barrier_semaphore()
    for d in range(1, n):
        pl.semaphore_signal(
            barrier, inc=1, device_id={"ctx": lax.rem(me + d, n)}, device_id_type=MESH
        )
    pl.semaphore_signal(barrier, inc=1, device_id=sibling, device_id_type=MESH)
    pl.semaphore_wait(barrier, n)

    def base(chunk):
        return pl.multiple_of(PAD + chunk * rows, 16)

    def source(d):
        return lax.rem(me + n - d, n)

    def peer(d):
        return {"ctx": lax.rem(me + d, n)}

    my_half = pl.multiple_of(core * half, 16)
    sends = []
    for d in range(1, n):
        copy = pltpu.make_async_remote_copy(
            src_ref=own_hbm.at[pl.ds(my_half, half)],
            dst_ref=hid.at[pl.ds(pl.multiple_of(base(me) + my_half, 16), half)],
            send_sem=hs_sem.at[d],
            recv_sem=hr_sem.at[d],
            device_id=peer(d),
            device_id_type=MESH,
        )
        copy.start()
        sends.append(copy)
    id_sends = []
    for d, slot in ((1, 0), (n - 1, 2)):
        copy = pltpu.make_async_remote_copy(
            src_ref=ids_hbm,
            dst_ref=ids.at[slot],
            send_sem=is_sem.at[d],
            recv_sem=ir_sem.at[d],
            device_id=peer(d),
            device_id_type=MESH,
        )
        copy.start()
        id_sends.append(copy)

    for edge in (0, PAD + total):
        hid[edge : edge + PAD] = jnp.zeros((PAD, width), BF16)
        q_all[edge : edge + PAD] = jnp.zeros((PAD, cols), BF16)

    def project(chunk):
        x = hid[pl.ds(base(chunk), rows)]
        at = pl.ds(pl.multiple_of(chunk * rows, 16), rows)
        q_all[pl.ds(base(chunk), rows)] = (nn(x, wqkv[0]).astype(BF16).astype(F32) * 0.125).astype(
            BF16
        )
        k_all[at] = nn(x, wqkv[1]).astype(BF16)
        v_all[at] = nn(x, wqkv[2]).astype(BF16)

    for load in loads[:3]:
        load.wait()
    project(me)
    forwards = []
    for d in range(1, n):
        sends[d - 1].wait_recv()
        block = hid.at[pl.ds(pl.multiple_of(base(source(d)) + my_half, 16), half)]
        copy = pltpu.make_async_remote_copy(
            src_ref=block,
            dst_ref=block,
            send_sem=fs_sem.at[d],
            recv_sem=fr_sem.at[d],
            device_id=sibling,
            device_id_type=MESH,
        )
        copy.start()
        forwards.append(copy)
    for d in range(1, n):
        forwards[d - 1].wait_recv()
        project(source(d))

    low = lax.broadcasted_iota(jnp.int32, (1, 128), 1) < 64
    low16 = jnp.where(low, 1.0, 0.0).astype(BF16)
    high16 = jnp.where(low, 0.0, 1.0).astype(BF16)
    usable = 4 * lax.broadcasted_iota(jnp.int32, (1, total), 1) < length

    def softmax_rows(q, k):
        scores = jnp.where(usable, nt(q, k), -1e30)
        largest = jnp.max(scores, axis=1, keepdims=True)
        weights = jnp.exp(scores - largest)
        totals = jnp.sum(weights, axis=1, keepdims=True)
        return weights, largest, totals

    window = pl.ds(pl.multiple_of(me * rows, 16), rows + 2 * PAD)

    def trimmed(x):
        return x.astype(F32)[PAD - HALO : PAD - HALO + win]

    q_win = trimmed(q_all[window]).astype(BF16)
    parts = []
    for pair in range(pairs):
        at = slice(128 * pair, 128 * pair + 128)
        q, k, v = q_win[:, at], k_all[:, at], v_all[:, at]
        outs = []
        for j, mask in enumerate((low16, high16)):
            weights, largest, totals = softmax_rows(q * mask, k)
            inverse = 1.0 / totals
            outs.append(nn(weights.astype(BF16), v) * inverse)
            p_own[2 * pair + j] = (weights * inverse)[HALO : HALO + rows]
        parts.append(jnp.where(low, outs[0], outs[1]).astype(BF16))
    loads[3].wait()

    swaps = []

    def swap(tx, rx, at):
        copy = pltpu.make_async_remote_copy(
            src_ref=tx.at[at],
            dst_ref=rx.at[at],
            send_sem=xs_sem.at[len(swaps)],
            recv_sem=xr_sem.at[len(swaps)],
            device_id=sibling,
            device_id_type=MESH,
        )
        copy.start()
        swaps.append(copy)
        return copy

    attn_win = jnp.concatenate(parts, axis=1)
    blocks = [slice(at, at + 256) for at in range(0, width, 256)]
    for i, at in enumerate(blocks):
        tx_attn[i] = nn(attn_win, wout[:, at])
        swap(tx_attn, rx_attn, i)
    def document_forward(pair):
        at = slice(128 * pair, 128 * pair + 128)
        q, k, v = q_all[PAD : PAD + total, at], k_all[:, at], v_all[:, at]
        outs, norms = [], []
        for mask in (low16, high16):
            weights, largest, totals = softmax_rows(q * mask, k)
            outs.append(nn(weights.astype(BF16), v) * (1.0 / totals))
            norms.append(largest + jnp.log(totals))
        attn_all[:, at] = jnp.where(low, outs[0], outs[1]).astype(BF16)
        ln2[pair] = jnp.where(low, norms[0], norms[1])

    for pair in range(pairs - 1):
        document_forward(pair)
    loads[4].wait()
    loads[5].wait()
    for copy in swaps:
        copy.wait_recv()
    first = me * rows - HALO
    place = first + lax.broadcasted_iota(jnp.int32, (win, 1), 0)
    inside = jnp.logical_and(place >= 0, place < total)
    added = [tx_attn[i] + rx_attn[i] for i in range(len(blocks))]
    context = trimmed(hid[window]) + jnp.concatenate(added, axis=1)
    context = jnp.where(inside, context, 0.0).astype(BF16)
    y0, y1, y2, y3 = [nn(context, wup[tap]) for tap in range(4)]

    def earlier(x):
        return pltpu.roll(x, 1, 0)

    def later(x):
        return pltpu.roll(x, win - 1, 0)

    y01, y23 = y0 + y1, y2 + y3
    pre = (earlier(y0) + y1 + y23, y01 + y23, y01 + y2 + later(y3), y01 + later(y23))
    c0, c1 = 0.7978845608028654, 0.044715
    log_swaps = []
    for phase in range(4):
        x = pre[phase]
        square = x * x
        th = jnp.tanh(c0 * (x + c1 * (x * square)))
        gate = 0.5 * (1.0 + th)
        active = (x * gate).astype(BF16)
        at = slice(phase * win, phase * win + win)
        tx_log[phase] = nn(active, whead[...])
        log_swaps.append(swap(tx_log, rx_log, phase))
        dgelu[at] = gate + 0.5 * x * (1.0 - th * th) * (c0 * (1.0 + 3.0 * c1 * square))
    own_keys = pl.ds(pl.multiple_of(me * rows, 16), rows)
    key_place = me * rows + lax.broadcasted_iota(jnp.int32, (1, 128), 1) % rows
    key_usable = 4 * key_place < length
    def key_probs(pair):
        at = slice(128 * pair, 128 * pair + 128)
        k = k_all[own_keys, at]
        both = jnp.concatenate([k * low16, k * high16], axis=0)
        scores = nt(q_all[PAD : PAD + total, at], both)
        p_keys[pair] = jnp.where(key_usable, jnp.exp(scores - ln2[pair]), 0.0)

    for pair in range(pairs - 1):
        key_probs(pair)
    for copy in id_sends:
        copy.wait_recv()
    byte = 4 * (lax.broadcasted_iota(jnp.int32, (win, 4 * rows), 0) - HALO)
    offset = byte - lax.broadcasted_iota(jnp.int32, (win, 4 * rows), 1)
    ids_win = []
    for phase in range(4):
        found = jnp.zeros((win, 4 * rows), jnp.int32)
        for side in range(3):
            found = found + jnp.where(offset == 4 * rows * (side - 1) - phase, ids[side], 0)
        ids_win.append(jnp.sum(found.astype(F32), axis=1, keepdims=True))
    inv_length = 1.0 / jnp.full((1, 1), length, jnp.int32).astype(F32)
    vocab = lax.broadcasted_iota(jnp.int32, (win, whead.shape[1]), 1).astype(F32)
    grads = []
    for phase in range(4):
        at = slice(phase * win, phase * win + win)
        log_swaps[phase].wait_recv()
        logits = tx_log[phase] + rx_log[phase]
        weights = jnp.exp(logits - jnp.max(logits, axis=1, keepdims=True))
        soft = weights * (1.0 / jnp.sum(weights, axis=1, keepdims=True))
        hot = jnp.where(vocab == ids_win[phase], 1.0, 0.0)
        counted = jnp.logical_and(inside, 4 * place + phase < length)
        logit_grad = ((soft - hot) * jnp.where(counted, inv_length, 0.0)).astype(BF16)
        grad = nt(logit_grad, whead[...]) * dgelu[at]
        grads.append(grad.astype(BF16).astype(F32))
    g0, g1, g2, g3 = grads
    g01, g23 = g0 + g1, g2 + g3
    taps = (later(g0) + g1 + g23, g01 + g23, earlier(g3) + g01 + g2, earlier(g23) + g01)
    taps = [x[HALO : HALO + rows].astype(BF16) for x in taps]
    ctx_swaps = []
    for i, at in enumerate(blocks):
        tx_ctx[i] = (nt(taps[0], wup[0, at]) + nt(taps[1], wup[1, at])) + (
            nt(taps[2], wup[2, at]) + nt(taps[3], wup[3, at])
        )
        ctx_swaps.append(swap(tx_ctx, rx_ctx, i))
    document_forward(pairs - 1)
    key_probs(pairs - 1)
    for copy in ctx_swaps:
        copy.wait_recv()
    context_grad = jnp.concatenate([tx_ctx[i] + rx_ctx[i] for i in range(len(blocks))], axis=1)
    ag = nt(context_grad.astype(BF16), wout[...]).astype(BF16)
    ag_all[own_keys] = ag
    ag_sends = []
    for d in range(1, n):
        block = ag_all.at[own_keys]
        copy = pltpu.make_async_remote_copy(
            src_ref=block,
            dst_ref=block,
            send_sem=as_sem.at[d],
            recv_sem=ar_sem.at[d],
            device_id=peer(d),
            device_id_type=MESH,
        )
        copy.start()
        ag_sends.append(copy)

    def head_dots(product):
        first_head = jnp.sum(jnp.where(low, product, 0.0), axis=1, keepdims=True)
        second_head = jnp.sum(jnp.where(low, 0.0, product), axis=1, keepdims=True)
        return first_head, second_head

    q_grads = []
    for pair in range(pairs):
        at = slice(128 * pair, 128 * pair + 128)
        g, k, v = ag[:, at], k_all[:, at], v_all[:, at]
        dots = head_dots(g.astype(F32) * attn_all[own_keys, at].astype(F32))
        outs = []
        for j, mask in enumerate((low16, high16)):
            score_grad = p_own[2 * pair + j] * (nt(g * mask, v) - dots[j])
            outs.append(nn(score_grad.astype(BF16), k))
        q_grads.append((jnp.where(low, outs[0], outs[1]) * 0.125).astype(BF16))
    back = nt(jnp.concatenate(q_grads, axis=1), wqkv[0])
    v_pairs = []
    for pair in range(pairs):
        v = v_all[own_keys, 128 * pair : 128 * pair + 128]
        v_pairs.append(jnp.concatenate([v * low16, v * high16], axis=0))
    k_sums = [jnp.zeros((128, 128), F32) for _ in range(pairs)]
    v_sums = [jnp.zeros((128, 128), F32) for _ in range(pairs)]
    for d in range(n):
        if d > 0:
            ag_sends[d - 1].wait_recv()
        chunk = source(d) if d > 0 else me
        block = pl.ds(pl.multiple_of(chunk * rows, 16), rows)
        for pair in range(pairs):
            at = slice(128 * pair, 128 * pair + 128)
            g = ag_all[block, at]
            dots = head_dots(g.astype(F32) * attn_all[block, at].astype(F32))
            probs = p_keys[pair, block]
            score_grad = probs * (nt(g, v_pairs[pair]) - jnp.where(low, dots[0], dots[1]))
            q = q_all[pl.ds(base(chunk), rows), at]
            k_sums[pair] = k_sums[pair] + tn(score_grad.astype(BF16), q)
            v_sums[pair] = v_sums[pair] + tn(probs.astype(BF16), g)

    def joined(sums):
        return jnp.concatenate(
            [jnp.where(low, s[:rows], s[rows:]).astype(BF16) for s in sums], axis=1
        )

    k_grad, v_grad = joined(k_sums), joined(v_sums)
    out_swaps = []
    for i, at in enumerate(blocks):
        tx_out[i] = back[:, at] + nt(k_grad, wqkv[1, at]) + nt(v_grad, wqkv[2, at])
        out_swaps.append(swap(tx_out, rx_out, i))
    for copy in sends + forwards + id_sends + ag_sends + swaps:
        copy.wait_send()
    for i, at in enumerate(blocks):
        out_swaps[i].wait_recv()
        out_ref[:, at] = (context_grad[:, at] + (tx_out[i] + rx_out[i])).astype(BF16)


def fused_body(byte_ids, lengths, hidden, w_qkv, w_out, w_up, w_head):
    n = lax.axis_size("ctx")
    rows, width = hidden.shape[1:]
    total = n * rows
    cols = w_out.shape[0]
    vocab = w_head.shape[1]
    win = rows + 2 * HALO
    vmem = pl.BlockSpec(memory_space=pltpu.VMEM)
    anywhere = pl.BlockSpec(memory_space=pl.ANY)
    dma = pltpu.SemaphoreType.DMA
    result = pl.pallas_call(
        functools.partial(kernel, n),
        out_shape=jax.ShapeDtypeStruct((rows, width), BF16),
        in_specs=[pl.BlockSpec(memory_space=pltpu.SMEM)] + [anywhere] * 6,
        out_specs=vmem,
        scratch_shapes=[
            pltpu.VMEM((3, 1, 4 * rows), jnp.int32),
            pltpu.VMEM((3, width, cols), BF16),
            pltpu.VMEM((cols, width), BF16),
            pltpu.VMEM((4, width, cols), BF16),
            pltpu.VMEM((cols, vocab), BF16),
            pltpu.VMEM((total + 2 * PAD, width), BF16),
            pltpu.VMEM((total + 2 * PAD, cols), BF16),
            pltpu.VMEM((total, cols), BF16),
            pltpu.VMEM((total, cols), BF16),
            pltpu.VMEM((total, cols), BF16),
            pltpu.VMEM((cols // 128, total, 128), F32),
            pltpu.VMEM((cols // 64, rows, total), F32),
            pltpu.VMEM((cols // 128, total, 128), F32),
            pltpu.VMEM((4 * win, cols), F32),
            pltpu.VMEM((total, cols), BF16),
            pltpu.VMEM((width // 256, win, 256), F32),
            pltpu.VMEM((width // 256, win, 256), F32),
            pltpu.VMEM((4, win, vocab), F32),
            pltpu.VMEM((4, win, vocab), F32),
            pltpu.VMEM((width // 256, rows, 256), F32),
            pltpu.VMEM((width // 256, rows, 256), F32),
            pltpu.VMEM((width // 256, rows, 256), F32),
            pltpu.VMEM((width // 256, rows, 256), F32),
            dma((6,)),
        ]
        + [dma((n,))] * 8
        + [dma((3 * (width // 256) + 4,))] * 2,
        compiler_params=pltpu.CompilerParams(
            collective_id=0, has_side_effects=True, vmem_limit_bytes=60 * 1024 * 1024
        ),
    )(
        lengths,
        byte_ids,
        hidden[0],
        jnp.transpose(w_qkv, (1, 0, 2)),
        w_out,
        w_up,
        w_head,
    )
    return result[None]


def fits(mesh, rows, width, cols):
    return 3 <= mesh.shape["ctx"] <= 4 and rows == 64 and cols % 128 == 0 and width % 256 == 0 and mesh.shape["mp"] == 2


def solution(mesh):
    def body(*arrays):
        (_, rows, width), cols = arrays[2].shape, arrays[4].shape[0]
        chosen = fused_body if fits(mesh, rows, width, cols) else general_body
        return chosen(*arrays)

    placed = (
        P(("groups", "dp"), "ctx"),
        P(("groups", "dp")),
        P(("groups", "dp"), "ctx", None),
        P(None, None, "mp"),
        P("mp", None),
        P(None, None, "mp"),
        P("mp", None),
    )
    return jax.shard_map(
        body,
        mesh=mesh,
        in_specs=placed,
        out_specs=P(("groups", "dp"), "ctx", None),
        check_vma=False,
    )
```
